128 devices in a mesh: wide: 16 (over x, z), narrow: 8 (over y, core).
Axes of the slice: x: 4, y: 4, z: 4, core: 2. Of those that a mesh axis runs over, the one named last changes fastest.
Arguments:
- tensor: bfloat16 [16, 128, 64, 16, 128], P('wide', None, 'narrow'), may hold values from -6 to 6
- tensor_mask: int32 [16, 16], P('wide'), may hold values 0 or 1
- occ_density: bfloat16 [16, 128, 16, 128], P('wide', None, 'narrow'), may hold values from -0.125 to 0.125
- occ_mask: int32 [16, 16], P('wide', 'narrow'), may hold values 0 or 1
- virt_density: bfloat16 [16, 128, 16, 128], P('wide', None, 'narrow'), may hold values from -0.125 to 0.125
- virt_mask: int32 [16, 16], P('wide', 'narrow'), may hold values 0 or 1
Outputs:
- contracted: bfloat16 [16, 128, 64, 16, 128], P(None, None, 'narrow', 'wide')
The draws below stay inside these ranges and needn't reach their ends.
All inputs are finite; a program needn't handle non-finite values. No bound on the sum of `tensor_mask` or of `occ_mask` or of `virt_mask` on one device may be relied on, other than what follows from the above.
Results may differ from the reference program's by a relative error of at most 0.0049.
Values may be sent and summed in bfloat16 or wider, within the bound.
A program may use at most 128 MiB of HBM per device.

```python
import jax
import jax.numpy as jnp
from jax import lax

BS = 128
NB = 16
PTOT = 64


def touch_ends(entries, rng, smallest, largest):
    longest = entries.shape.index(max(entries.shape))
    spots = []
    for shift in (0, 1):
        where = [jax.random.randint(jax.random.fold_in(rng, axis), (), 0, length) for axis, length in enumerate(entries.shape)]
        where[longest] = (where[longest] + shift) % entries.shape[longest]
        spots.append(tuple(where))
    return entries.at[spots[0]].set(smallest).at[spots[1]].set(largest)


def block_scale(own_key, extent, split, low, high):
    factor_of = 1.0
    for dim, parts in split:
        heights = jax.random.uniform(jax.random.fold_in(jax.random.fold_in(own_key, 6), dim), (parts,), jnp.float32, low / len(split), high / len(split))
        factor_of = factor_of * jnp.repeat(jnp.exp(heights), extent[dim] // parts).reshape((-1,) + (1,) * (len(extent) - 1 - dim))
    return factor_of


def normal_values(rng, shape, width, reach, split=(), held_as=jnp.bfloat16):
    array = jax.random.normal(rng, shape, jnp.float32) * width
    if len(split) > 0:
        array = block_scale(rng, shape, split, -0.22, 0.18) * array
    return jnp.clip(array, min=-reach, max=reach).astype(held_as)


def setup_inputs(seed: int = 0) -> dict:
    streams_of = jax.random.split(jax.random.key(seed), 7)
    return {
        "tensor": normal_values(streams_of[0], (NB, BS, PTOT, NB, BS), 1.0, 6.0, ((0, 16), (2, 8))),
        "tensor_mask": touch_ends((jax.random.randint(streams_of[1], (NB, NB), 0, 4) < 3).astype(jnp.int32), jax.random.fold_in(streams_of[1], 1), 0, 1),
        "occ_density": normal_values(streams_of[2], (NB, BS, NB, BS), (NB * BS) ** -0.5, 0.125, ((0, 16), (2, 8))),
        "occ_mask": touch_ends((jax.random.randint(streams_of[3], (NB, NB), 0, 4) < 3).astype(jnp.int32), jax.random.fold_in(streams_of[3], 1), 0, 1),
        "virt_density": normal_values(streams_of[4], (NB, BS, NB, BS), (NB * BS) ** -0.5, 0.125, ((0, 16), (2, 8))),
        "virt_mask": touch_ends((jax.random.randint(streams_of[5], (NB, NB), 0, 4) < 3).astype(jnp.int32), jax.random.fold_in(streams_of[5], 1), 0, 1),
    }


def reference(tensor, tensor_mask, occ_density, occ_mask, virt_density, virt_mask):
    block_count = tensor.shape[0]
    block_size = tensor.shape[1]
    rank_total = tensor.shape[2]
    occ_blocks = occ_density * occ_mask.astype(occ_density.dtype)[:, None, :, None]
    occ_flat = occ_blocks.reshape(block_count * block_size, block_count * block_size)
    virt_blocks = virt_density * virt_mask.astype(virt_density.dtype)[:, None, :, None]
    virt_flat = virt_blocks.reshape(block_count * block_size, block_count * block_size)

    def first_pass(pair):
        block_row, row_mask = pair
        masked = block_row * row_mask.astype(block_row.dtype)[None, None, :, None]
        product = jnp.dot(masked.reshape(block_size * rank_total, block_count * block_size), occ_flat, preferred_element_type=jnp.float32)
        return product.astype(jnp.bfloat16).reshape(block_size, rank_total, block_count, block_size)

    half_moved = lax.map(first_pass, (tensor, tensor_mask))
    by_rank = jnp.moveaxis(half_moved, 2, 0)

    def second_pass(slab):
        product = jnp.dot(virt_flat, slab.reshape(block_count * block_size, block_count * block_size), preferred_element_type=jnp.float32)
        return product.astype(jnp.bfloat16).reshape(block_count, block_size, block_count, block_size)

    result_slabs = lax.map(second_pass, by_rank)
    return jnp.moveaxis(result_slabs, 0, 2)
```

```python
import functools

import jax
import jax.numpy as jnp
from jax import lax
from jax.experimental import pallas as pl
from jax.experimental.pallas import tpu as pltpu
from jax.sharding import PartitionSpec as P

MESH = pl.DeviceIdType.MESH
BF16 = jnp.bfloat16
F32 = jnp.float32
S = 128
NB = 16
PL = 8
ROUNDS = 4
ROWS = 2 * PL * S


def ring(v):
    return lax.rem(v + 4, 4)


def kernel(
    t_hbm, tmask, occ_ref, omask, virt_ref, vmask, out_hbm,
    traw, tm, occ, acc, send, recv, virt, outv, perm,
    t_sem, x_ssem, x_rsem, o1_ssem, o1_rsem, o_ssem, o_rsem,
    v1_ssem, v1_rsem, v2_ssem, v2_rsem, v3_ssem, v3_rsem,
    a_ssem, a_rsem, out_sem,
):
    w = lax.axis_index("wide")
    n = lax.axis_index("narrow")
    x, z = w // 4, lax.rem(w, 4)
    y, k = n // 2, lax.rem(n, 2)

    def remote(src, dst, ssem, rsem, wide, narrow):
        return pltpu.make_async_remote_copy(
            src_ref=src, dst_ref=dst, send_sem=ssem, recv_sem=rsem,
            device_id=(wide, narrow), device_id_type=MESH,
        )

    def wait_rows(sem, rows):
        view = virt.at[pl.ds(0, rows), :]
        pltpu.make_async_copy(view, view, sem).wait()

    barrier = pltpu.get_barrier_semaphore()
    for d in range(1, 4):
        pl.semaphore_signal(barrier, inc=1, device_id=(w, ring(y + d) * 2 + k), device_id_type=MESH)
    for d in range(1, 16):
        for e in range(2):
            pl.semaphore_signal(
                barrier, inc=1, device_id=(lax.rem(w + d, 16), y * 2 + e), device_id_type=MESH
            )
    pl.semaphore_signal(barrier, inc=1, device_id=(w, y * 2 + 1 - k), device_id_type=MESH)

    for p in range(PL):
        pltpu.make_async_copy(t_hbm.at[:, p], traw.at[p], t_sem.at[p]).start()

    ycol = pl.ds(pl.multiple_of(y * S, S), S)
    ncol = pl.ds(pl.multiple_of(n * 2 * S, 2 * S), 2 * S)
    wrow = pl.ds(pl.multiple_of(w * S, S), S)
    for j in range(2):
        block = occ_ref[:, j, :].astype(F32) * omask[0, j].astype(F32)
        occ[j, w, :, ycol] = block.astype(BF16)
    for j in range(2):
        block = virt_ref[:, j, :].astype(F32) * vmask[0, j].astype(F32)
        virt[wrow, pl.ds(pl.multiple_of(n * 2 * S + j * S, S), S)] = block.astype(BF16)

    row = lax.broadcasted_iota(jnp.int32, (256, 256), 0)
    col = lax.broadcasted_iota(jnp.int32, (256, 256), 1)
    scale = jnp.zeros((256, 256), F32)
    for b in range(NB):
        scale = scale + jnp.where((row >> 4) == b, 1.0, 0.0) * tmask[0, b].astype(F32)
    hit = jnp.logical_and((row >> 4) == (col & 15), (row & 15) == (col >> 4))
    perm[...] = jnp.where(hit, scale, 0.0).astype(BF16)

    pl.semaphore_wait(barrier, 34)

    for d in (1, 3, 2):
        for i in range(2):
            own = occ.at[i, w, :, ycol]
            remote(own, own, o1_ssem, o1_rsem, w, ring(y + d) * 2 + k).start()
    for d in range(1, 16):
        own = virt.at[wrow, ncol]
        remote(own, own, v1_ssem, v1_rsem, lax.rem(w + d, 16), n).start()

    def own_rows(r):
        return pl.ds(pl.multiple_of(r * 512 + k * 256, 256), 256)

    def relayout(r):
        for pi in range(2):
            p = 2 * r + pi
            pltpu.make_async_copy(t_hbm.at[:, p], traw.at[p], t_sem.at[p]).wait()

            def body(g, c, p=p, pi=pi):
                pair = jnp.concatenate(
                    [
                        traw[p, pl.ds(pl.multiple_of(g * 32 + h * 16, 16), 16)].reshape(256, S)
                        for h in range(2)
                    ],
                    axis=1,
                )
                got = jnp.dot(perm[...], pair, preferred_element_type=F32).astype(BF16)
                for h in range(2):
                    first = r * 512 + k * 256 + pi * S + g * 32 + h * 16
                    tm[:, pl.ds(pl.multiple_of(first, 16), 16), :] = got[:, h * S : (h + 1) * S].reshape(
                        NB, 16, S
                    )
                return c

            lax.fori_loop(0, 4, body, 0)
        mine = tm.at[:, own_rows(r), :]
        remote(mine, mine, x_ssem.at[r], x_rsem.at[r], w, y * 2 + 1 - k).start()

    relayout(0)

    place = ((x, z), (z, x))

    def at(i, p, q):
        return p * 4 + q if i == 0 else q * 4 + p

    def pass_block(i, b, p, q):
        remote(occ.at[i, b], occ.at[i, b], o_ssem, o_rsem.at[i, b], at(i, p, q), n).start()

    def wait_block(i, b):
        pltpu.make_async_copy(occ.at[i, b], occ.at[i, b], o_rsem.at[i, b]).wait()

    wait_rows(o1_rsem, 48)
    for d in (1, 3, 2):
        for i in range(2):
            p, q = place[i]
            pass_block(i, w, ring(p + d), q)
    for i in range(2):
        p, q = place[i]
        for d in (1, 3):
            pass_block(i, w, p, ring(q + d))

    relayout(1)
    for d in (1, 3, 2):
        for i in range(2):
            p, q = place[i]
            b = at(i, ring(p + d), q)
            wait_block(i, b)
            for f in (1, 3):
                pass_block(i, b, p, ring(q + f))
    relayout(2)
    relayout(3)

    halves = [pl.ds(0, ROWS // 2), pl.ds(ROWS // 2, ROWS // 2)]

    def columns(yy, kk):
        return pl.ds(pl.multiple_of((yy * 2 + kk) * 2 * S, 2 * S), 2 * S)

    def to_core(yy, h):
        part = virt.at[halves[h], columns(yy, k)]
        remote(part, part, v3_ssem, v3_rsem, w, y * 2 + 1 - k).start()

    def along(yy, h, d, s):
        part = virt.at[halves[h], columns(yy, k)]
        remote(part, part, v2_ssem.at[s], v2_rsem.at[lax.rem(yy, 4), h], w, ring(y + d) * 2 + k).start()

    def wait_along(yy, h):
        part = virt.at[halves[h], columns(yy, k)]
        pltpu.make_async_copy(part, part, v2_rsem.at[yy, h]).wait()

    wait_rows(v1_rsem, 15 * 16)
    along(y, 0, 3, 0)
    along(y, 1, 1, 1)
    along(y, 1, 3, 2)
    along(y, 0, 1, 3)
    to_core(y, 0)
    to_core(y, 1)

    def product(i, bs, rows):
        lhs = jnp.concatenate([tm[b, rows, :] for b in bs], axis=1)
        rhs = jnp.concatenate([occ[i, b] for b in bs], axis=0)
        return jnp.dot(lhs, rhs, preferred_element_type=F32)

    def group(i, d):
        p, q = place[i]
        return [at(i, ring(p + f), ring(q + d)) for f in range(4)]

    def accumulate(d, first, cores):
        def body(r, c):
            for e in cores:
                rows = pl.ds(pl.multiple_of(r * 512 + e * 256, 256), 256)
                for i in range(2):
                    got = product(i, group(i, d), rows)
                    acc[i, rows, :] = got if first else acc[i, rows, :] + got
            return c

        lax.fori_loop(0, ROUNDS, body, 0)

    accumulate(0, True, [k])
    for i in range(2):
        p, q = place[i]
        for f in (0, 1):
            b = at(i, ring(p + f), ring(q + 1))
            wait_block(i, b)
            pass_block(i, b, p, ring(q + 3))
        for f in (3, 2):
            b = at(i, ring(p + f), ring(q + 3))
            wait_block(i, b)
            pass_block(i, b, p, ring(q + 1))
    for r in range(ROUNDS):
        theirs = tm.at[:, pl.ds(pl.multiple_of(r * 512 + (1 - k) * 256, 256), 256), :]
        pltpu.make_async_copy(theirs, theirs, x_rsem.at[r]).wait()
    accumulate(0, True, [1 - k])
    for i in range(2):
        p, q = place[i]
        for f in (3, 2):
            wait_block(i, at(i, ring(p + f), ring(q + 1)))
    accumulate(1, False, [0, 1])
    for i in range(2):
        p, q = place[i]
        for f in (0, 1):
            wait_block(i, at(i, ring(p + f), ring(q + 3)))
    accumulate(3, False, [0, 1])
    for i in range(2):
        p, q = place[i]
        for f in range(4):
            wait_block(i, at(i, ring(p + f), ring(q + 2)))

    def finish(r, c):
        for i in range(2):
            for e in range(2):
                rows = pl.ds(pl.multiple_of(r * 512 + e * 256, 256), 256)
                got = (acc[i, rows, :] + product(i, group(i, 2), rows)).astype(BF16)
                for xx in range(4):
                    for pi in range(2):
                        send[r, i, xx, e, :, pi * S : (pi + 1) * S] = got[
                            pi * S : (pi + 1) * S, xx * S : (xx + 1) * S
                        ]
        for d in (1, 3, 2, 0):
            xx = ring(x + d)
            for j in range(2):
                i = lax.rem(j + z, 2)
                for e in range(2):
                    wide = xx * 4 + 2 * k + i
                    here = jnp.logical_and(wide == w, k == e)
                    src = send.at[r, i, xx, e]
                    dst = recv.at[r, wrow, :]

                    def away(src=src, dst=dst, wide=wide, e=e):
                        remote(src, dst, a_ssem.at[r], a_rsem.at[r], wide, y * 2 + e).start()

                    if d == 0:
                        pl.when(jnp.logical_not(here))(away)

                        @pl.when(here)
                        def _(src=src, dst=dst):
                            pltpu.make_async_copy(src, dst, a_rsem.at[r]).start()
                    else:
                        away()
        return c

    lax.fori_loop(0, ROUNDS, finish, 0)

    up, down, far = ring(y + 1), ring(y + 3), ring(y + 2)
    wait_along(up, 0)
    along(up, 0, 3, 4)
    to_core(up, 0)
    wait_along(down, 1)
    along(down, 1, 1, 5)
    to_core(down, 1)
    wait_along(up, 1)
    to_core(up, 1)
    wait_along(down, 0)
    to_core(down, 0)
    wait_along(far, 0)
    to_core(far, 0)
    wait_along(far, 1)
    to_core(far, 1)
    wait_rows(v3_rsem, ROWS // 2)

    def second(r, c):
        pltpu.make_async_copy(recv.at[r], recv.at[r], a_rsem.at[r]).wait()

        def chunk(m, cc):
            rows = pl.ds(pl.multiple_of(m * 256, 256), 256)
            got = jnp.dot(virt[rows, :], recv[r], preferred_element_type=F32).astype(BF16)
            for pi in range(2):
                outv[2 * r + pi, rows, :] = got[:, pi * S : (pi + 1) * S]
            part = outv.at[pl.ds(2 * r, 2), rows, :]
            pltpu.make_async_copy(part, out_hbm.at[pl.ds(2 * r, 2), rows, :], out_sem).start()
            return cc

        lax.fori_loop(0, 8, chunk, 0)
        return c

    lax.fori_loop(0, ROUNDS, second, 0)

    pltpu.make_async_copy(outv, out_hbm, out_sem).wait()
    wait_rows(o1_ssem, 48)
    wait_rows(o_ssem, 960)
    wait_rows(v1_ssem, 15 * 16)
    for s in range(6):
        part = virt.at[halves[0], pl.ds(0, 2 * S)]
        pltpu.make_async_copy(part, part, v2_ssem.at[s]).wait()
    wait_rows(v3_ssem, ROWS // 2)
    for r in range(ROUNDS):
        mine = tm.at[:, own_rows(r), :]
        pltpu.make_async_copy(mine, mine, x_ssem.at[r]).wait()
        local = z // 2 == k

        @pl.when(local)
        def _(r=r):
            wait_rows(a_ssem.at[r], 15 * 16)

        @pl.when(jnp.logical_not(local))
        def _(r=r):
            wait_rows(a_ssem.at[r], 16 * 16)


def shards(tensor, tensor_mask, occ_density, occ_mask, virt_density, virt_mask):
    dma = pltpu.SemaphoreType.DMA
    vmem, smem = pl.BlockSpec(memory_space=pltpu.VMEM), pl.BlockSpec(memory_space=pltpu.SMEM)
    out = pl.pallas_call(
        kernel,
        out_shape=jax.ShapeDtypeStruct((PL, NB * S, S), BF16),
        in_specs=[pl.BlockSpec(memory_space=pl.ANY), smem, vmem, smem, vmem, smem],
        out_specs=pl.BlockSpec(memory_space=pl.ANY),
        scratch_shapes=[
            pltpu.VMEM((PL, S, NB, S), BF16),
            pltpu.VMEM((NB, ROWS, S), BF16),
            pltpu.VMEM((2, NB, S, 4 * S), BF16),
            pltpu.VMEM((2, ROWS, 4 * S), F32),
            pltpu.VMEM((ROUNDS, 2, 4, 2, S, 2 * S), BF16),
            pltpu.VMEM((ROUNDS, NB * S, 2 * S), BF16),
            pltpu.VMEM((NB * S, NB * S), BF16),
            pltpu.VMEM((PL, NB * S, S), BF16),
            pltpu.VMEM((256, 256), BF16),
            dma((PL,)),
            dma((ROUNDS,)), dma((ROUNDS,)),
            dma(()), dma(()),
            dma(()), dma((2, NB)),
            dma(()), dma(()),
            dma((6,)), dma((4, 2)),
            dma(()), dma(()),
            dma((ROUNDS,)), dma((ROUNDS,)),
            dma(()),
        ],
        compiler_params=pltpu.CompilerParams(
            collective_id=0, has_side_effects=True, vmem_limit_bytes=56 << 20
        ),
        cost_estimate=pl.CostEstimate(flops=17 << 30, bytes_accessed=8 << 20, transcendentals=0),
    )(
        tensor.reshape(S, PL, NB, S), tensor_mask,
        occ_density.reshape(S, 2, S), occ_mask, virt_density.reshape(S, 2, S), virt_mask,
    )
    return jnp.transpose(out, (1, 0, 2)).reshape(NB, S, PL, 1, S)


def solution(mesh):
    placed = (
        P("wide", None, "narrow", None, None),
        P("wide", None),
        P("wide", None, "narrow", None),
        P("wide", "narrow"),
        P("wide", None, "narrow", None),
        P("wide", "narrow"),
    )
    return jax.shard_map(
        shards,
        mesh=mesh,
        in_specs=placed,
        out_specs=P(None, None, "narrow", "wide", None),
        check_vma=False,
    )
```

```python
import functools

import jax
import jax.numpy as jnp
from jax import lax
from jax.experimental import pallas as pl
from jax.experimental.pallas import tpu as pltpu
from jax.sharding import PartitionSpec as P

MESH = pl.DeviceIdType.MESH
BF16 = jnp.bfloat16
F32 = jnp.float32
S = 128
NB = 16
PL = 8
ROUNDS = 4
ROWS = 2 * PL * S
NA = 80
NC = S - NA


NEAR = (
    (1, 0), (0, 1), (3, 0), (0, 3), (1, 1), (3, 3), (1, 3), (3, 1),
    (2, 0), (0, 2), (2, 1), (1, 2), (2, 3), (3, 2), (2, 2),
)


def ring(v):
    return lax.rem(v + 4, 4)


def kernel(
    t_hbm, tmask, occ_ref, omask, virt_ref, vmask, out_hbm,
    traw, tm, occ, send, recv, virt, stage, outv, perm,
    t_sem, x_ssem, x_rsem, o1_ssem, o1_rsem, o2_ssem, o3_ssem, o_rsem, c1_ssem, c1_rsem, c2_ssem, c2_rsem,
    v1_ssem, v1_rsem, v1b_ssem, v1b_rsem, v2_ssem, v2_rsem, v3_ssem, v3_rsem,
    a_ssem, a_rsem, out_sem,
):
    w = lax.axis_index("wide")
    n = lax.axis_index("narrow")
    x, z = w // 4, lax.rem(w, 4)
    y, k = n // 2, lax.rem(n, 2)

    def remote(src, dst, ssem, rsem, wide, narrow):
        return pltpu.make_async_remote_copy(
            src_ref=src, dst_ref=dst, send_sem=ssem, recv_sem=rsem,
            device_id=(wide, narrow), device_id_type=MESH,
        )

    def wait_kib(sem, kib):
        view = recv.at[0, pl.ds(0, kib * 2), :] if kib < 1024 else tm.at[pl.ds(0, kib // 4), :]
        pltpu.make_async_copy(view, view, sem).wait()

    barrier = pltpu.get_barrier_semaphore()
    for d in range(1, 4):
        pl.semaphore_signal(barrier, inc=1, device_id=(w, ring(y + d) * 2 + k), device_id_type=MESH)
    for d in range(1, 16):
        for e in range(2):
            pl.semaphore_signal(
                barrier, inc=1, device_id=(lax.rem(w + d, 16), y * 2 + e), device_id_type=MESH
            )
    pl.semaphore_signal(barrier, inc=1, device_id=(w, y * 2 + 1 - k), device_id_type=MESH)

    for p in range(PL):
        pltpu.make_async_copy(t_hbm.at[:, p], traw.at[p], t_sem.at[p]).start()

    ycol = pl.ds(pl.multiple_of(y * S, S), S)
    ncol = pl.ds(pl.multiple_of(n * 2 * S, 2 * S), 2 * S)
    wrow = pl.ds(pl.multiple_of(w * S, S), S)
    for j in range(2):
        block = occ_ref[:, j, :].astype(F32) * omask[0, j].astype(F32)
        occ[j, w, :, ycol] = block.astype(BF16)
    for j in range(2):
        block = virt_ref[:, j, :].astype(F32) * vmask[0, j].astype(F32)
        virt[x, z, :, pl.ds(pl.multiple_of(n * 2 * S + j * S, S), S)] = block.astype(BF16)

    row = lax.broadcasted_iota(jnp.int32, (256, 256), 0)
    col = lax.broadcasted_iota(jnp.int32, (256, 256), 1)
    scale = jnp.zeros((256, 256), F32)
    for b in range(NB):
        scale = scale + jnp.where((row >> 4) == b, 1.0, 0.0) * tmask[0, b].astype(F32)
    hit = jnp.logical_and((row >> 4) == (col & 15), (row & 15) == (col >> 4))
    perm[...] = jnp.where(hit, scale, 0.0).astype(BF16)

    pl.semaphore_wait(barrier, 34)

    first, other = pl.ds(0, NA), pl.ds(NA, NC)
    for d in (1, 3, 2):
        for i in range(2):
            own = occ.at[i, w, first, ycol]
            remote(own, own, o1_ssem, o1_rsem, w, ring(y + d) * 2 + k).start()
    for dx, dz in NEAR:
        own = occ.at[:, w, other, ycol]
        remote(own, own, c1_ssem, c1_rsem, ring(x + dx) * 4 + ring(z + dz), n).start()
    place = ((x, z), (z, x))

    def at(i, p, q):
        return p * 4 + q if i == 0 else q * 4 + p

    upper, lower = pl.ds(0, S // 2), pl.ds(S // 2, S // 2)
    for d in (1, 3, 2):
        for i, part in enumerate((upper, lower)):
            p, q = place[i]
            own = virt.at[x, z, part, ncol]
            remote(own, own, v1_ssem, v1_rsem, at(i, ring(p + d), q), n).start()

    def own_rows(r):
        return pl.ds(pl.multiple_of(r * 512 + k * 256, 256), 256)

    def relayout(r):
        for pi in range(2):
            p = 2 * r + pi
            pltpu.make_async_copy(t_hbm.at[:, p], traw.at[p], t_sem.at[p]).wait()

            def body(g, c, p=p, pi=pi):
                pair = jnp.concatenate(
                    [
                        traw[p, pl.ds(pl.multiple_of(g * 32 + h * 16, 16), 16)].reshape(256, S)
                        for h in range(2)
                    ],
                    axis=1,
                )
                got = jnp.dot(perm[...], pair, preferred_element_type=F32).astype(BF16)
                for h in range(2):
                    top = r * 512 + k * 256 + pi * S + g * 32 + h * 16
                    for b in range(NB):
                        tm[pl.ds(pl.multiple_of(top, 16), 16), b * S : (b + 1) * S] = got[
                            b * 16 : (b + 1) * 16, h * S : (h + 1) * S
                        ]
                return c

            lax.fori_loop(0, 4, body, 0)
        mine = tm.at[own_rows(r), :]
        remote(mine, mine, x_ssem.at[r], x_rsem.at[r], w, y * 2 + 1 - k).start()

    relayout(0)

    def pass_block(i, b, p, q, ssem=o3_ssem):
        part = occ.at[i, b, first, :]
        remote(part, part, ssem, o_rsem.at[i, b], at(i, p, q), n).start()

    def wait_block(i, b):
        part = occ.at[i, b, first, :]
        pltpu.make_async_copy(part, part, o_rsem.at[i, b]).wait()

    def spread(i, yy, d):
        part = occ.at[i, :, other, pl.ds(pl.multiple_of(yy * S, S), S)]
        remote(part, part, c2_ssem, c2_rsem.at[yy, i], w, ring(y + d) * 2 + k).start()

    def wait_spread(i, yy):
        part = occ.at[i, :, other, pl.ds(pl.multiple_of(yy * S, S), S)]
        pltpu.make_async_copy(part, part, c2_rsem.at[yy, i]).wait()

    up, down, far = ring(y + 1), ring(y + 3), ring(y + 2)

    wait_kib(o1_rsem, 6 * NA // 4)
    for d in (1, 3, 2):
        for i in range(2):
            p, q = place[i]
            pass_block(i, w, ring(p + d), q, o2_ssem)
    for i in range(2):
        p, q = place[i]
        for d in (1, 3):
            pass_block(i, w, p, ring(q + d))

    wait_kib(c1_rsem, 15 * NC // 2)
    for i, d in ((0, 3), (1, 1), (0, 1), (1, 3)):
        spread(i, y, d)

    wait_kib(v1_rsem, 192)
    for d in (1, 3, 2):
        for i, part in enumerate((virt.at[:, z, upper, ncol], virt.at[x, :, lower, ncol])):
            p, q = place[i]
            remote(part, part, v1b_ssem, v1b_rsem, at(i, p, ring(q + d)), n).start()

    relayout(1)
    for d in (1, 3, 2):
        for i in range(2):
            p, q = place[i]
            b = at(i, ring(p + d), q)
            wait_block(i, b)
            for f in (1, 3):
                pass_block(i, b, p, ring(q + f))
    relayout(2)
    wait_spread(0, up)
    spread(0, up, 3)
    wait_spread(1, down)
    spread(1, down, 1)
    for f, g in ((0, 3), (1, 2)):
        for i in range(2):
            p, q = place[i]
            for dq, dp, to in ((1, f, 3), (3, g, 1)):
                b = at(i, ring(p + dp), ring(q + dq))
                wait_block(i, b)
                pass_block(i, b, p, ring(q + to))
        if f == 0:
            relayout(3)

    halves = [pl.ds(0, 2), pl.ds(2, 2)]

    def columns(yy, kk):
        return pl.ds(pl.multiple_of((yy * 2 + kk) * 2 * S, 2 * S), 2 * S)

    def to_core(yy, h):
        part = virt.at[halves[h], :, :, columns(yy, k)]
        remote(part, part, v3_ssem, v3_rsem, w, y * 2 + 1 - k).start()

    def along(yy, h, d, s):
        part = virt.at[halves[h], :, :, columns(yy, k)]
        remote(part, part, v2_ssem.at[s], v2_rsem.at[lax.rem(yy, 4), h], w, ring(y + d) * 2 + k).start()

    def wait_along(yy, h):
        part = virt.at[halves[h], :, :, columns(yy, k)]
        pltpu.make_async_copy(part, part, v2_rsem.at[yy, h]).wait()

    wait_kib(v1b_rsem, 768)
    along(y, 0, 3, 0)
    along(y, 1, 1, 1)
    along(y, 1, 3, 2)
    along(y, 0, 1, 3)
    to_core(y, 0)
    to_core(y, 1)

    for r in range(ROUNDS):
        theirs = tm.at[pl.ds(pl.multiple_of(r * 512 + (1 - k) * 256, 256), 256), :]
        pltpu.make_async_copy(theirs, theirs, x_rsem.at[r]).wait()
    for i in range(2):
        p, q = place[i]
        for dq, dp in ((1, 3), (1, 2), (3, 0), (3, 1), (2, 0), (2, 1), (2, 2), (2, 3)):
            wait_block(i, at(i, ring(p + dp), ring(q + dq)))
        for yy in (far, up if i == 1 else down):
            wait_spread(i, yy)

    def first_product(r, c):
        for j in range(2):
            i = lax.rem(j + z, 2)
            for e in range(2):
                rows = pl.ds(pl.multiple_of(r * 512 + e * 256, 256), 256)
                got = jnp.dot(
                    tm[rows, :], occ[i].reshape(NB * S, 4 * S), preferred_element_type=F32
                ).astype(BF16)
                for xx in range(4):
                    for pi in range(2):
                        send[r, i, xx, e, :, pi * S : (pi + 1) * S] = got[
                            pi * S : (pi + 1) * S, xx * S : (xx + 1) * S
                        ]
            for d in (1, 3, 2, 0):
                xx = ring(x + d)
                for e in range(2):
                    wide = xx * 4 + 2 * k + i
                    here = jnp.logical_and(wide == w, k == e)
                    src = send.at[r, i, xx, e]
                    dst = recv.at[r, wrow, :]

                    def away(src=src, dst=dst, wide=wide, e=e):
                        remote(src, dst, a_ssem.at[r], a_rsem.at[r], wide, y * 2 + e).start()

                    if d == 0:
                        pl.when(jnp.logical_not(here))(away)

                        @pl.when(here)
                        def _(src=src, dst=dst):
                            pltpu.make_async_copy(src, dst, a_rsem.at[r]).start()
                    else:
                        away()
        return c

    lax.fori_loop(0, ROUNDS, first_product, 0)

    wait_along(up, 0)
    along(up, 0, 3, 4)
    to_core(up, 0)
    wait_along(down, 1)
    along(down, 1, 1, 5)
    to_core(down, 1)
    wait_along(up, 1)
    to_core(up, 1)
    wait_along(down, 0)
    to_core(down, 0)
    wait_along(far, 0)
    to_core(far, 0)
    wait_along(far, 1)
    to_core(far, 1)
    wait_kib(v3_rsem, 4096)

    def second(r, last):
        pltpu.make_async_copy(recv.at[r], recv.at[r], a_rsem.at[r]).wait()

        def chunk(m, c):
            rows = pl.ds(pl.multiple_of(m * 256, 256), 256)
            lhs = virt[m // 2, pl.ds(lax.rem(m, 2) * 2, 2)].reshape(256, NB * S)
            got = jnp.dot(lhs, recv[r], preferred_element_type=F32)
            for pi in range(2):
                stage[rows, 2 * r + pi, :] = got[:, pi * S : (pi + 1) * S]
            if last:
                outv[rows] = stage[rows].astype(BF16)
                pltpu.make_async_copy(outv.at[rows], out_hbm.at[rows], out_sem).start()
            return c

        lax.fori_loop(0, 8, chunk, 0)

    for r in range(ROUNDS):
        second(r, r == ROUNDS - 1)

    pltpu.make_async_copy(outv, out_hbm, out_sem).wait()
    wait_kib(o1_ssem, 6 * NA // 4)
    wait_kib(o2_ssem, 6 * NA)
    wait_kib(o3_ssem, 24 * NA)
    wait_kib(c1_ssem, 15 * NC // 2)
    wait_kib(c2_ssem, 24 * NC)
    wait_kib(v1_ssem, 192)
    wait_kib(v1b_ssem, 768)
    for t in range(6):
        wait_kib(v2_ssem.at[t], 512)
    wait_kib(v3_ssem, 4096)
    for r in range(ROUNDS):
        mine = tm.at[own_rows(r), :]
        pltpu.make_async_copy(mine, mine, x_ssem.at[r]).wait()
        local = z // 2 == k

        @pl.when(local)
        def _(r=r):
            wait_kib(a_ssem.at[r], 960)

        @pl.when(jnp.logical_not(local))
        def _(r=r):
            wait_kib(a_ssem.at[r], 1024)


def shards(tensor, tensor_mask, occ_density, occ_mask, virt_density, virt_mask):
    dma = pltpu.SemaphoreType.DMA
    vmem, smem = pl.BlockSpec(memory_space=pltpu.VMEM), pl.BlockSpec(memory_space=pltpu.SMEM)
    out = pl.pallas_call(
        kernel,
        out_shape=jax.ShapeDtypeStruct((NB * S, PL, S), BF16),
        in_specs=[pl.BlockSpec(memory_space=pl.ANY), smem, vmem, smem, vmem, smem],
        out_specs=pl.BlockSpec(memory_space=pl.ANY),
        scratch_shapes=[
            pltpu.VMEM((PL, S, NB, S), BF16),
            pltpu.VMEM((ROWS, NB * S), BF16),
            pltpu.VMEM((2, NB, S, 4 * S), BF16),
            pltpu.VMEM((ROUNDS, 2, 4, 2, S, 2 * S), BF16),
            pltpu.VMEM((ROUNDS, NB * S, 2 * S), BF16),
            pltpu.VMEM((4, 4, S, NB * S), BF16),
            pltpu.VMEM((NB * S, PL, S), F32),
            pltpu.VMEM((NB * S, PL, S), BF16),
            pltpu.VMEM((256, 256), BF16),
            dma((PL,)),
            dma((ROUNDS,)), dma((ROUNDS,)),
            dma(()), dma(()),
            dma(()), dma(()), dma((2, NB)),
            dma(()), dma(()), dma(()), dma((4, 2)),
            dma(()), dma(()),
            dma(()), dma(()),
            dma((6,)), dma((4, 2)),
            dma(()), dma(()),
            dma((ROUNDS,)), dma((ROUNDS,)),
            dma(()),
        ],
        compiler_params=pltpu.CompilerParams(
            collective_id=0, has_side_effects=True, vmem_limit_bytes=56 << 20
        ),
        cost_estimate=pl.CostEstimate(flops=17 << 30, bytes_accessed=8 << 20, transcendentals=0),
    )(
        tensor.reshape(S, PL, NB, S), tensor_mask,
        occ_density.reshape(S, 2, S), occ_mask, virt_density.reshape(S, 2, S), virt_mask,
    )
    return out.reshape(NB, S, PL, 1, S)


def solution(mesh):
    placed = (
        P("wide", None, "narrow", None, None),
        P("wide", None),
        P("wide", None, "narrow", None),
        P("wide", "narrow"),
        P("wide", None, "narrow", None),
        P("wide", "narrow"),
    )
    return jax.shard_map(
        shards,
        mesh=mesh,
        in_specs=placed,
        out_specs=P(None, None, "narrow", "wide", None),
        check_vma=False,
    )
```

```python
import functools

import jax
import jax.numpy as jnp
from jax import lax
from jax.experimental import pallas as pl
from jax.experimental.pallas import tpu as pltpu
from jax.sharding import PartitionSpec as P

MESH = pl.DeviceIdType.MESH
BF16 = jnp.bfloat16
F32 = jnp.float32
S = 128
NB = 16
PL = 8
ROUNDS = 4
ROWS = 2 * PL * S
NA = 80
NC = S - NA
VMEM_LIMIT = 43 << 20
LAST_LIMIT = 8 << 20
CHUNK = 512


NEAR = (
    (1, 0), (0, 1), (3, 0), (0, 3), (1, 1), (3, 3), (1, 3), (3, 1),
    (2, 0), (0, 2), (2, 1), (1, 2), (2, 3), (3, 2), (2, 2),
)


def ring(v):
    return lax.rem(v + 4, 4)


def second_product(virt, recv, stage, r, m, c):
    rows = pl.ds(pl.multiple_of(m * CHUNK, CHUNK), CHUNK)
    per = CHUNK // S
    lhs = virt[m * per // 4, pl.ds(lax.rem(m * per, 4), per)].reshape(CHUNK, NB * S)
    got = jnp.dot(lhs, recv[r], preferred_element_type=F32)
    for pi in range(2):
        stage[rows, 2 * r + pi, :] = got[:, pi * S : (pi + 1) * S]
    return c


def last_kernel(virt, recv, stage, out_hbm, outv, out_sem):
    def body(m, c):
        second_product(virt, recv, stage, ROUNDS - 1, m, c)
        rows = pl.ds(pl.multiple_of(m * CHUNK, CHUNK), CHUNK)
        outv[rows] = stage[rows].astype(BF16)
        pltpu.make_async_copy(outv.at[rows], out_hbm.at[rows], out_sem).start()
        return c

    lax.fori_loop(0, NB * S // CHUNK, body, 0)
    pltpu.make_async_copy(outv, out_hbm, out_sem).wait()


def kernel(
    t_hbm, tmask, occ_ref, omask, virt_ref, vmask, virt, recv, stage,
    traw, tm, occ, send, perm,
    t_sem, x_ssem, x_rsem, o1_ssem, o1_rsem, o2_ssem, o3_ssem, o_rsem, c1_ssem, c1_rsem, c2_ssem, c2_rsem,
    v1_ssem, v1_rsem, v1b_ssem, v1b_rsem, v2_ssem, v2_rsem, v3_ssem, v3_rsem,
    a_ssem, a_rsem,
):
    w = lax.axis_index("wide")
    n = lax.axis_index("narrow")
    x, z = w // 4, lax.rem(w, 4)
    y, k = n // 2, lax.rem(n, 2)

    def remote(src, dst, ssem, rsem, wide, narrow):
        return pltpu.make_async_remote_copy(
            src_ref=src, dst_ref=dst, send_sem=ssem, recv_sem=rsem,
            device_id=(wide, narrow), device_id_type=MESH,
        )

    def wait_kib(sem, kib):
        view = recv.at[0, pl.ds(0, kib * 2), :] if kib < 1024 else tm.at[pl.ds(0, kib // 4), :]
        pltpu.make_async_copy(view, view, sem).wait()

    barrier = pltpu.get_barrier_semaphore()
    for d in range(1, 4):
        pl.semaphore_signal(barrier, inc=1, device_id=(w, ring(y + d) * 2 + k), device_id_type=MESH)
    for d in range(1, 16):
        for e in range(2):
            pl.semaphore_signal(
                barrier, inc=1, device_id=(lax.rem(w + d, 16), y * 2 + e), device_id_type=MESH
            )
    pl.semaphore_signal(barrier, inc=1, device_id=(w, y * 2 + 1 - k), device_id_type=MESH)

    for p in range(PL):
        pltpu.make_async_copy(t_hbm.at[:, p], traw.at[p], t_sem.at[p]).start()

    ycol = pl.ds(pl.multiple_of(y * S, S), S)
    ncol = pl.ds(pl.multiple_of(n * 2 * S, 2 * S), 2 * S)
    wrow = pl.ds(pl.multiple_of(w * S, S), S)
    for j in range(2):
        block = occ_ref[:, j, :].astype(F32) * omask[0, j].astype(F32)
        occ[j, w, :, ycol] = block.astype(BF16)
    for j in range(2):
        block = virt_ref[:, j, :].astype(F32) * vmask[0, j].astype(F32)
        virt[x, z, :, pl.ds(pl.multiple_of(n * 2 * S + j * S, S), S)] = block.astype(BF16)

    row = lax.broadcasted_iota(jnp.int32, (256, 256), 0)
    col = lax.broadcasted_iota(jnp.int32, (256, 256), 1)
    scale = jnp.zeros((256, 256), F32)
    for b in range(NB):
        scale = scale + jnp.where((row >> 4) == b, 1.0, 0.0) * tmask[0, b].astype(F32)
    hit = jnp.logical_and((row >> 4) == (col & 15), (row & 15) == (col >> 4))
    perm[...] = jnp.where(hit, scale, 0.0).astype(BF16)

    pl.semaphore_wait(barrier, 34)

    first, other = pl.ds(0, NA), pl.ds(NA, NC)
    for d in (1, 3, 2):
        for i in range(2):
            own = occ.at[i, w, first, ycol]
            remote(own, own, o1_ssem, o1_rsem, w, ring(y + d) * 2 + k).start()
    for dx, dz in NEAR:
        own = occ.at[:, w, other, ycol]
        remote(own, own, c1_ssem, c1_rsem, ring(x + dx) * 4 + ring(z + dz), n).start()
    place = ((x, z), (z, x))

    def at(i, p, q):
        return p * 4 + q if i == 0 else q * 4 + p

    upper, lower = pl.ds(0, S // 2), pl.ds(S // 2, S // 2)
    for d in (1, 3, 2):
        for i, part in enumerate((upper, lower)):
            p, q = place[i]
            own = virt.at[x, z, part, ncol]
            remote(own, own, v1_ssem, v1_rsem, at(i, ring(p + d), q), n).start()

    def own_rows(r):
        return pl.ds(pl.multiple_of(r * 512 + k * 256, 256), 256)

    def relayout(r):
        for pi in range(2):
            p = 2 * r + pi
            pltpu.make_async_copy(t_hbm.at[:, p], traw.at[p], t_sem.at[p]).wait()

            def body(g, c, p=p, pi=pi):
                pair = jnp.concatenate(
                    [
                        traw[p, pl.ds(pl.multiple_of(g * 32 + h * 16, 16), 16)].reshape(256, S)
                        for h in range(2)
                    ],
                    axis=1,
                )
                got = jnp.dot(perm[...], pair, preferred_element_type=F32).astype(BF16)
                for h in range(2):
                    top = r * 512 + k * 256 + pi * S + g * 32 + h * 16
                    for b in range(NB):
                        tm[pl.ds(pl.multiple_of(top, 16), 16), b * S : (b + 1) * S] = got[
                            b * 16 : (b + 1) * 16, h * S : (h + 1) * S
                        ]
                return c

            lax.fori_loop(0, 4, body, 0)
        mine = tm.at[own_rows(r), :]
        remote(mine, mine, x_ssem.at[r], x_rsem.at[r], w, y * 2 + 1 - k).start()

    relayout(0)

    def pass_block(i, b, p, q, ssem=o3_ssem):
        part = occ.at[i, b, first, :]
        remote(part, part, ssem, o_rsem.at[i, b], at(i, p, q), n).start()

    def wait_block(i, b):
        part = occ.at[i, b, first, :]
        pltpu.make_async_copy(part, part, o_rsem.at[i, b]).wait()

    def spread(i, yy, d):
        part = occ.at[i, :, other, pl.ds(pl.multiple_of(yy * S, S), S)]
        remote(part, part, c2_ssem, c2_rsem.at[yy, i], w, ring(y + d) * 2 + k).start()

    def wait_spread(i, yy):
        part = occ.at[i, :, other, pl.ds(pl.multiple_of(yy * S, S), S)]
        pltpu.make_async_copy(part, part, c2_rsem.at[yy, i]).wait()

    up, down, far = ring(y + 1), ring(y + 3), ring(y + 2)

    wait_kib(o1_rsem, 6 * NA // 4)
    for d in (1, 3, 2):
        for i in range(2):
            p, q = place[i]
            pass_block(i, w, ring(p + d), q, o2_ssem)
    for i in range(2):
        p, q = place[i]
        for d in (1, 3):
            pass_block(i, w, p, ring(q + d))

    wait_kib(c1_rsem, 15 * NC // 2)
    for i, d in ((0, 3), (1, 1), (0, 1), (1, 3)):
        spread(i, y, d)

    wait_kib(v1_rsem, 192)
    for d in (1, 3, 2):
        for i, part in enumerate((virt.at[:, z, upper, ncol], virt.at[x, :, lower, ncol])):
            p, q = place[i]
            remote(part, part, v1b_ssem, v1b_rsem, at(i, p, ring(q + d)), n).start()

    relayout(1)
    for d in (1, 3, 2):
        for i in range(2):
            p, q = place[i]
            b = at(i, ring(p + d), q)
            wait_block(i, b)
            for f in (1, 3):
                pass_block(i, b, p, ring(q + f))
    relayout(2)
    wait_spread(0, up)
    spread(0, up, 3)
    wait_spread(1, down)
    spread(1, down, 1)
    for f, g in ((0, 3), (1, 2)):
        for i in range(2):
            p, q = place[i]
            for dq, dp, to in ((1, f, 3), (3, g, 1)):
                b = at(i, ring(p + dp), ring(q + dq))
                wait_block(i, b)
                pass_block(i, b, p, ring(q + to))
        if f == 0:
            relayout(3)

    halves = [pl.ds(0, 2), pl.ds(2, 2)]

    def columns(yy, kk):
        return pl.ds(pl.multiple_of((yy * 2 + kk) * 2 * S, 2 * S), 2 * S)

    def to_core(yy, h):
        part = virt.at[halves[h], :, :, columns(yy, k)]
        remote(part, part, v3_ssem, v3_rsem, w, y * 2 + 1 - k).start()

    def along(yy, h, d, s):
        part = virt.at[halves[h], :, :, columns(yy, k)]
        remote(part, part, v2_ssem.at[s], v2_rsem.at[lax.rem(yy, 4), h], w, ring(y + d) * 2 + k).start()

    def wait_along(yy, h):
        part = virt.at[halves[h], :, :, columns(yy, k)]
        pltpu.make_async_copy(part, part, v2_rsem.at[yy, h]).wait()

    wait_kib(v1b_rsem, 768)
    along(y, 0, 3, 0)
    along(y, 1, 1, 1)
    along(y, 1, 3, 2)
    along(y, 0, 1, 3)
    to_core(y, 0)
    to_core(y, 1)

    for r in range(ROUNDS):
        theirs = tm.at[pl.ds(pl.multiple_of(r * 512 + (1 - k) * 256, 256), 256), :]
        pltpu.make_async_copy(theirs, theirs, x_rsem.at[r]).wait()
    for i in range(2):
        p, q = place[i]
        for dq, dp in ((1, 3), (1, 2), (3, 0), (3, 1), (2, 0), (2, 1), (2, 2), (2, 3)):
            wait_block(i, at(i, ring(p + dp), ring(q + dq)))
        for yy in (far, up if i == 1 else down):
            wait_spread(i, yy)

    def first_product(r, c):
        for j in range(2):
            i = lax.rem(j + z, 2)
            for e in range(2):
                rows = pl.ds(pl.multiple_of(r * 512 + e * 256, 256), 256)
                got = jnp.dot(
                    tm[rows, :], occ[i].reshape(NB * S, 4 * S), preferred_element_type=F32
                ).astype(BF16)
                for xx in range(4):
                    for pi in range(2):
                        send[r, i, xx, e, :, pi * S : (pi + 1) * S] = got[
                            pi * S : (pi + 1) * S, xx * S : (xx + 1) * S
                        ]
            for d in (1, 3, 2, 0):
                xx = ring(x + d)
                for e in range(2):
                    wide = xx * 4 + 2 * k + i
                    here = jnp.logical_and(wide == w, k == e)
                    src = send.at[r, i, xx, e]
                    dst = recv.at[r, wrow, :]

                    def away(src=src, dst=dst, wide=wide, e=e):
                        remote(src, dst, a_ssem.at[r], a_rsem.at[r], wide, y * 2 + e).start()

                    if d == 0:
                        pl.when(jnp.logical_not(here))(away)

                        @pl.when(here)
                        def _(src=src, dst=dst):
                            pltpu.make_async_copy(src, dst, a_rsem.at[r]).start()
                    else:
                        away()
        return c

    lax.fori_loop(0, ROUNDS, first_product, 0)

    wait_along(up, 0)
    along(up, 0, 3, 4)
    to_core(up, 0)
    wait_along(down, 1)
    along(down, 1, 1, 5)
    to_core(down, 1)
    wait_along(up, 1)
    to_core(up, 1)
    wait_along(down, 0)
    to_core(down, 0)
    wait_along(far, 0)
    to_core(far, 0)
    wait_along(far, 1)
    to_core(far, 1)
    wait_kib(v3_rsem, 4096)

    for r in range(ROUNDS):
        pltpu.make_async_copy(recv.at[r], recv.at[r], a_rsem.at[r]).wait()
        if r < ROUNDS - 1:
            lax.fori_loop(0, NB * S // CHUNK, functools.partial(second_product, virt, recv, stage, r), 0)

    wait_kib(o1_ssem, 6 * NA // 4)
    wait_kib(o2_ssem, 6 * NA)
    wait_kib(o3_ssem, 24 * NA)
    wait_kib(c1_ssem, 15 * NC // 2)
    wait_kib(c2_ssem, 24 * NC)
    wait_kib(v1_ssem, 192)
    wait_kib(v1b_ssem, 768)
    for t in range(6):
        wait_kib(v2_ssem.at[t], 512)
    wait_kib(v3_ssem, 4096)
    for r in range(ROUNDS):
        mine = tm.at[own_rows(r), :]
        pltpu.make_async_copy(mine, mine, x_ssem.at[r]).wait()
        local = z // 2 == k

        @pl.when(local)
        def _(r=r):
            wait_kib(a_ssem.at[r], 960)

        @pl.when(jnp.logical_not(local))
        def _(r=r):
            wait_kib(a_ssem.at[r], 1024)


def shards(tensor, tensor_mask, occ_density, occ_mask, virt_density, virt_mask):
    dma = pltpu.SemaphoreType.DMA
    vmem, smem = pl.BlockSpec(memory_space=pltpu.VMEM), pl.BlockSpec(memory_space=pltpu.SMEM)
    virt, recv, stage = pl.pallas_call(
        kernel,
        out_shape=[
            pltpu.VMEM((4, 4, S, NB * S), BF16),
            pltpu.VMEM((ROUNDS, NB * S, 2 * S), BF16),
            pltpu.VMEM((NB * S, PL, S), F32),
        ],
        in_specs=[pl.BlockSpec(memory_space=pl.ANY), smem, vmem, smem, vmem, smem],
        out_specs=[vmem] * 3,
        scratch_shapes=[
            pltpu.VMEM((PL, S, NB, S), BF16),
            pltpu.VMEM((ROWS, NB * S), BF16),
            pltpu.VMEM((2, NB, S, 4 * S), BF16),
            pltpu.VMEM((ROUNDS, 2, 4, 2, S, 2 * S), BF16),
            pltpu.VMEM((256, 256), BF16),
            dma((PL,)),
            dma((ROUNDS,)), dma((ROUNDS,)),
            dma(()), dma(()),
            dma(()), dma(()), dma((2, NB)),
            dma(()), dma(()), dma(()), dma((4, 2)),
            dma(()), dma(()),
            dma(()), dma(()),
            dma((6,)), dma((4, 2)),
            dma(()), dma(()),
            dma((ROUNDS,)), dma((ROUNDS,)),
        ],
        compiler_params=pltpu.CompilerParams(
            collective_id=0, has_side_effects=True, vmem_limit_bytes=VMEM_LIMIT
        ),
        cost_estimate=pl.CostEstimate(flops=15 << 30, bytes_accessed=8 << 20, transcendentals=0),
    )(
        tensor.reshape(S, PL, NB, S), tensor_mask,
        occ_density.reshape(S, 2, S), occ_mask, virt_density.reshape(S, 2, S), virt_mask,
    )
    out = pl.pallas_call(
        last_kernel,
        out_shape=jax.ShapeDtypeStruct((NB * S, PL, S), BF16),
        in_specs=[vmem] * 3,
        out_specs=pl.BlockSpec(memory_space=pl.ANY),
        scratch_shapes=[pltpu.VMEM((NB * S, PL, S), BF16), dma(())],
        compiler_params=pltpu.CompilerParams(vmem_limit_bytes=LAST_LIMIT),
        cost_estimate=pl.CostEstimate(flops=2 << 30, bytes_accessed=4 << 20, transcendentals=0),
    )(virt, recv, stage)
    return out.reshape(NB, S, PL, 1, S)


def solution(mesh):
    placed = (
        P("wide", None, "narrow", None, None),
        P("wide", None),
        P("wide", None, "narrow", None),
        P("wide", "narrow"),
        P("wide", None, "narrow", None),
        P("wide", "narrow"),
    )
    return jax.shard_map(
        shards,
        mesh=mesh,
        in_specs=placed,
        out_specs=P(None, None, "narrow", "wide", None),
        check_vma=False,
    )
```

```python
import functools

import jax
import jax.numpy as jnp
from jax import lax
from jax.experimental import pallas as pl
from jax.experimental.pallas import tpu as pltpu
from jax.sharding import PartitionSpec as P

MESH = pl.DeviceIdType.MESH
BF16 = jnp.bfloat16
F32 = jnp.float32
S = 128
NB = 16
PL = 8
ROUNDS = 4
ROWS = 2 * PL * S
NA = 80
NC = S - NA
VMEM_LIMIT = 47 << 20
LAST_LIMIT = 8 << 20
CHUNK = 4 * S
HALF = NB * S // 2


NEAR = (
    (1, 0), (0, 1), (3, 0), (0, 3), (1, 1), (3, 3), (1, 3), (3, 1),
    (2, 0), (0, 2), (2, 1), (1, 2), (2, 3), (3, 2), (2, 2),
)


def ring(v):
    return lax.rem(v + 4, 4)


def chunk_rows(m):
    return pl.ds(pl.multiple_of(m * CHUNK, CHUNK), CHUNK)


def product(virt, recv, r, m):
    lhs = virt[m].reshape(CHUNK, NB * S)
    return jnp.dot(lhs, recv[r], preferred_element_type=F32).astype(BF16).reshape(CHUNK, 2, S)


def last_kernel(virt, recv, done, out_hbm, outv, out_sem):
    def body(m, c):
        rows = chunk_rows(m)
        outv[rows] = done[rows]
        outv[rows, PL - 2 : PL, :] = product(virt, recv, ROUNDS - 1, m)
        pltpu.make_async_copy(outv.at[rows], out_hbm.at[rows], out_sem).start()
        return c

    lax.fori_loop(0, NB * S // CHUNK, body, 0)
    pltpu.make_async_copy(outv, out_hbm, out_sem).wait()


def kernel(
    t_hbm, tmask_hbm, occ_hbm, omask_hbm, virt_hbm, vmask_hbm, virt, recv, done,
    tmask, occ_ref, omask, virt_ref, vmask, in_sem, traw, tm, occ, send, perm,
    t_sem, x_ssem, x_rsem, o1_ssem, o1_rsem, o2_ssem, o3_ssem, o_rsem, c1_ssem, c1_rsem, c2_ssem, c2_rsem,
    v1_ssem, v1_rsem, v1b_ssem, v1b_rsem, v2_ssem, v2_rsem, v3_ssem, v3_rsem,
    a_ssem, a_rsem,
):
    w = lax.axis_index("wide")
    n = lax.axis_index("narrow")
    x, z = w // 4, lax.rem(w, 4)
    y, k = n // 2, lax.rem(n, 2)

    def remote(src, dst, ssem, rsem, wide, narrow):
        return pltpu.make_async_remote_copy(
            src_ref=src, dst_ref=dst, send_sem=ssem, recv_sem=rsem,
            device_id=(wide, narrow), device_id_type=MESH,
        )

    def wait_kib(sem, kib):
        view = recv.at[0, pl.ds(0, kib * 2), :] if kib < 1024 else tm.at[pl.ds(0, kib // 4), :]
        pltpu.make_async_copy(view, view, sem).wait()

    barrier = pltpu.get_barrier_semaphore()
    for dx, dz in reversed(NEAR):
        for e in range(2):
            pl.semaphore_signal(
                barrier,
                inc=1,
                device_id=(ring(x + dx) * 4 + ring(z + dz), y * 2 + e),
                device_id_type=MESH,
            )
    for d in (2, 1, 3):
        pl.semaphore_signal(barrier, inc=1, device_id=(w, ring(y + d) * 2 + k), device_id_type=MESH)
    pl.semaphore_signal(barrier, inc=1, device_id=(w, y * 2 + 1 - k), device_id_type=MESH)

    inputs = [
        pltpu.make_async_copy(src, dst, in_sem.at[t])
        for t, (src, dst) in enumerate(
            (
                (omask_hbm, omask), (occ_hbm, occ_ref), (vmask_hbm, vmask),
                (virt_hbm, virt_ref), (tmask_hbm, tmask),
            )
        )
    ]
    for copy in inputs:
        copy.start()
    for p in range(PL):
        pltpu.make_async_copy(t_hbm.at[:, p], traw.at[p], t_sem.at[p]).start()
    inputs[0].wait()
    inputs[1].wait()

    ycol = pl.ds(pl.multiple_of(y * S, S), S)
    ncol = pl.ds(pl.multiple_of(n * 2 * S, 2 * S), 2 * S)
    wrow = pl.ds(pl.multiple_of(w * S, S), S)
    for j in range(2):
        block = occ_ref[:, j, :].astype(F32) * omask[0, j].astype(F32)
        occ[j, w, :, ycol] = block.astype(BF16)
    pl.semaphore_wait(barrier, 34)

    first, other = pl.ds(0, NA), pl.ds(NA, NC)
    for d in (1, 3, 2):
        for i in range(2):
            own = occ.at[i, w, first, ycol]
            remote(own, own, o1_ssem, o1_rsem, w, ring(y + d) * 2 + k).start()
    for dx, dz in NEAR:
        own = occ.at[:, w, other, ycol]
        remote(own, own, c1_ssem, c1_rsem, ring(x + dx) * 4 + ring(z + dz), n).start()
    inputs[2].wait()
    inputs[3].wait()
    for j in range(2):
        block = virt_ref[:, j, :].astype(F32) * vmask[0, j].astype(F32)
        virt[x, z, :, pl.ds(pl.multiple_of(n * 2 * S + j * S, S), S)] = block.astype(BF16)

    place = ((x, z), (z, x))

    def at(i, p, q):
        return p * 4 + q if i == 0 else q * 4 + p

    upper, lower = pl.ds(0, S // 2), pl.ds(S // 2, S // 2)
    for d in (1, 3, 2):
        for i, part in enumerate((upper, lower)):
            p, q = place[i]
            own = virt.at[x, z, part, ncol]
            remote(own, own, v1_ssem, v1_rsem, at(i, ring(p + d), q), n).start()

    inputs[4].wait()
    row = lax.broadcasted_iota(jnp.int32, (256, 256), 0)
    col = lax.broadcasted_iota(jnp.int32, (256, 256), 1)
    scale = jnp.zeros((256, 256), F32)
    for b in range(NB):
        scale = scale + jnp.where((row >> 4) == b, 1.0, 0.0) * tmask[0, b].astype(F32)
    hit = jnp.logical_and((row >> 4) == (col & 15), (row & 15) == (col >> 4))
    perm[...] = jnp.where(hit, scale, 0.0).astype(BF16)

    def own_rows(r):
        return pl.ds(pl.multiple_of(r * 512 + k * 256, 256), 256)

    def relayout(r):
        for pi in range(2):
            p = 2 * r + pi
            pltpu.make_async_copy(t_hbm.at[:, p], traw.at[p], t_sem.at[p]).wait()

            def body(g, c, p=p, pi=pi):
                pair = jnp.concatenate(
                    [
                        traw[p, pl.ds(pl.multiple_of(g * 32 + h * 16, 16), 16)].reshape(256, S)
                        for h in range(2)
                    ],
                    axis=1,
                )
                got = jnp.dot(perm[...], pair, preferred_element_type=F32).astype(BF16)
                for h in range(2):
                    top = r * 512 + k * 256 + pi * S + g * 32 + h * 16
                    for b in range(NB):
                        tm[pl.ds(pl.multiple_of(top, 16), 16), b * S : (b + 1) * S] = got[
                            b * 16 : (b + 1) * 16, h * S : (h + 1) * S
                        ]
                return c

            lax.fori_loop(0, 4, body, 0)
        mine = tm.at[own_rows(r), :]
        remote(mine, mine, x_ssem.at[r], x_rsem.at[r], w, y * 2 + 1 - k).start()

    relayout(0)

    def pass_block(i, b, p, q, ssem=o3_ssem):
        part = occ.at[i, b, first, :]
        remote(part, part, ssem, o_rsem.at[i, b], at(i, p, q), n).start()

    def wait_block(i, b):
        part = occ.at[i, b, first, :]
        pltpu.make_async_copy(part, part, o_rsem.at[i, b]).wait()

    def spread(i, yy, d):
        part = occ.at[i, :, other, pl.ds(pl.multiple_of(yy * S, S), S)]
        remote(part, part, c2_ssem, c2_rsem.at[yy, i], w, ring(y + d) * 2 + k).start()

    def wait_spread(i, yy):
        part = occ.at[i, :, other, pl.ds(pl.multiple_of(yy * S, S), S)]
        pltpu.make_async_copy(part, part, c2_rsem.at[yy, i]).wait()

    up, down, far = ring(y + 1), ring(y + 3), ring(y + 2)

    wait_kib(o1_rsem, 6 * NA // 4)
    for d in (1, 3, 2):
        for i in range(2):
            p, q = place[i]
            pass_block(i, w, ring(p + d), q, o2_ssem)
    for i in range(2):
        p, q = place[i]
        for d in (1, 3):
            pass_block(i, w, p, ring(q + d))

    wait_kib(c1_rsem, 15 * NC // 2)
    for i, d in ((0, 3), (1, 1), (0, 1), (1, 3)):
        spread(i, y, d)

    relayout(1)
    for d in (1, 3, 2):
        for i in range(2):
            p, q = place[i]
            b = at(i, ring(p + d), q)
            wait_block(i, b)
            for f in (1, 3):
                pass_block(i, b, p, ring(q + f))
    def line(i, q, h=None):
        part = pl.ds(0, 4) if h is None else pl.ds(2 * h, 2)
        return virt.at[part, q, upper, ncol] if i == 0 else virt.at[q, part, lower, ncol]

    def pass_line(i, q, d, t, h=None):
        ref = line(i, q, h)
        p, here = place[i]
        remote(ref, ref, v1b_ssem, v1b_rsem.at[i, t], at(i, p, ring(here + d)), n).start()

    def wait_line(i, q, t, h=None):
        ref = line(i, q, h)
        pltpu.make_async_copy(ref, ref, v1b_rsem.at[i, t]).wait()

    wait_kib(v1_rsem, 192)
    for i in range(2):
        q = place[i][1]
        pass_line(i, q, 3, 0)
        pass_line(i, q, 1, 1)

    wait_spread(0, up)
    spread(0, up, 3)
    wait_spread(1, down)
    spread(1, down, 1)
    for f, g in ((0, 3), (1, 2)):
        for i in range(2):
            p, q = place[i]
            for dq, dp, to in ((1, f, 3), (3, g, 1)):
                b = at(i, ring(p + dp), ring(q + dq))
                wait_block(i, b)
                pass_block(i, b, p, ring(q + to))

    halves = [pl.ds(0, 2), pl.ds(2, 2)]

    def columns(yy, kk):
        return pl.ds(pl.multiple_of((yy * 2 + kk) * 2 * S, 2 * S), 2 * S)

    def to_core(yy, h):
        part = virt.at[halves[h], :, :, columns(yy, k)]
        remote(part, part, v3_ssem, v3_rsem, w, y * 2 + 1 - k).start()

    def along(yy, h, d, s):
        part = virt.at[halves[h], :, :, columns(yy, k)]
        remote(part, part, v2_ssem.at[s], v2_rsem.at[lax.rem(yy, 4), h], w, ring(y + d) * 2 + k).start()

    def wait_along(yy, h):
        part = virt.at[halves[h], :, :, columns(yy, k)]
        pltpu.make_async_copy(part, part, v2_rsem.at[yy, h]).wait()

    for i in range(2):
        q = place[i][1]
        wait_line(i, ring(q + 1), 0)
        pass_line(i, ring(q + 1), 3, 2, 0)
        wait_line(i, ring(q + 3), 1)
        pass_line(i, ring(q + 3), 1, 3, 1)
    relayout(2)
    relayout(3)
    for i in range(2):
        p, q = place[i]
        for dq, dp in ((1, 3), (1, 2), (3, 0), (3, 1), (2, 0), (2, 1), (2, 2), (2, 3)):
            wait_block(i, at(i, ring(p + dp), ring(q + dq)))
        for yy in (far, up if i == 1 else down):
            wait_spread(i, yy)

    def first_product(r, c):
        theirs = tm.at[pl.ds(pl.multiple_of(r * 512 + (1 - k) * 256, 256), 256), :]
        pltpu.make_async_copy(theirs, theirs, x_rsem.at[r]).wait()
        for j in range(2):
            i = lax.rem(j + x // 2, 2)
            for e in range(2):
                rows = pl.ds(pl.multiple_of(r * 512 + e * 256, 256), 256)
                got = jnp.dot(
                    tm[rows, :], occ[i].reshape(NB * S, 4 * S), preferred_element_type=F32
                ).astype(BF16)
                for xx in range(4):
                    for pi in range(2):
                        send[r, i, xx, e, :, pi * S : (pi + 1) * S] = got[
                            pi * S : (pi + 1) * S, xx * S : (xx + 1) * S
                        ]
                for d in (1, 3, 2, 0):
                    xx = ring(x + d)
                    wide = xx * 4 + 2 * k + i
                    here = jnp.logical_and(wide == w, k == e)
                    src = send.at[r, i, xx, e]
                    dst = recv.at[r, wrow, :]
                    rsem = a_rsem.at[r, x // 2]

                    def away(src=src, dst=dst, rsem=rsem, wide=wide, e=e):
                        remote(src, dst, a_ssem.at[r], rsem, wide, y * 2 + e).start()

                    if d == 0:
                        pl.when(jnp.logical_not(here))(away)

                        @pl.when(here)
                        def _(src=src, dst=dst, rsem=rsem):
                            pltpu.make_async_copy(src, dst, rsem).start()
                    else:
                        away()
        return c

    first_product(0, 0)
    for i in range(2):
        q = place[i][1]
        for h in range(2):
            wait_line(i, ring(q + 2), 2 + h, h)
    along(y, 0, 3, 0)
    along(y, 1, 1, 1)
    along(y, 1, 3, 2)
    along(y, 0, 1, 3)
    to_core(y, 0)
    to_core(y, 1)

    lax.fori_loop(1, ROUNDS, first_product, 0)

    wait_along(up, 0)
    along(up, 0, 3, 4)
    to_core(up, 0)
    wait_along(down, 1)
    along(down, 1, 1, 5)
    to_core(down, 1)
    wait_along(up, 1)
    to_core(up, 1)
    wait_along(down, 0)
    to_core(down, 0)
    wait_along(far, 0)
    to_core(far, 0)
    wait_along(far, 1)
    to_core(far, 1)
    wait_kib(v3_rsem, 4096)

    def arrive(r, h):
        half = recv.at[r, pl.ds(pl.multiple_of(h * HALF, HALF), HALF), :]
        pltpu.make_async_copy(half, half, a_rsem.at[r, h]).wait()

    for r in range(ROUNDS - 1):
        arrive(r, 0)
        arrive(r, 1)

        def second_product(m, c, r=r):
            done[chunk_rows(m), 2 * r : 2 * r + 2, :] = product(virt, recv, r, m)
            return c

        lax.fori_loop(0, NB * S // CHUNK, second_product, 0)

    def wait_sent(r):
        local = z // 2 == k

        @pl.when(local)
        def _():
            wait_kib(a_ssem.at[r], 960)

        @pl.when(jnp.logical_not(local))
        def _():
            wait_kib(a_ssem.at[r], 1024)

    wait_kib(o1_ssem, 6 * NA // 4)
    wait_kib(o2_ssem, 6 * NA)
    wait_kib(o3_ssem, 24 * NA)
    wait_kib(c1_ssem, 15 * NC // 2)
    wait_kib(c2_ssem, 24 * NC)
    wait_kib(v1_ssem, 192)
    wait_kib(v1b_ssem, 768)
    for t in range(6):
        wait_kib(v2_ssem.at[t], 512)
    wait_kib(v3_ssem, 4096)
    for r in range(ROUNDS):
        mine = tm.at[own_rows(r), :]
        pltpu.make_async_copy(mine, mine, x_ssem.at[r]).wait()
        if r < ROUNDS - 1:
            wait_sent(r)

    arrive(ROUNDS - 1, 0)
    arrive(ROUNDS - 1, 1)
    wait_sent(ROUNDS - 1)


def shards(tensor, tensor_mask, occ_density, occ_mask, virt_density, virt_mask):
    dma = pltpu.SemaphoreType.DMA
    vmem, hbm = pl.BlockSpec(memory_space=pltpu.VMEM), pl.BlockSpec(memory_space=pl.ANY)
    virt, recv, done = pl.pallas_call(
        kernel,
        out_shape=[
            pltpu.VMEM((4, 4, S, NB * S), BF16),
            pltpu.VMEM((ROUNDS, NB * S, 2 * S), BF16),
            pltpu.VMEM((NB * S, PL, S), BF16),
        ],
        in_specs=[hbm] * 6,
        out_specs=[vmem] * 3,
        scratch_shapes=[
            pltpu.SMEM((1, NB), jnp.int32),
            pltpu.VMEM((S, 2, S), BF16),
            pltpu.SMEM((1, 2), jnp.int32),
            pltpu.VMEM((S, 2, S), BF16),
            pltpu.SMEM((1, 2), jnp.int32),
            dma((5,)),
            pltpu.VMEM((PL, S, NB, S), BF16),
            pltpu.VMEM((ROWS, NB * S), BF16),
            pltpu.VMEM((2, NB, S, 4 * S), BF16),
            pltpu.VMEM((ROUNDS, 2, 4, 2, S, 2 * S), BF16),
            pltpu.VMEM((256, 256), BF16),
            dma((PL,)),
            dma((ROUNDS,)), dma((ROUNDS,)),
            dma(()), dma(()),
            dma(()), dma(()), dma((2, NB)),
            dma(()), dma(()), dma(()), dma((4, 2)),
            dma(()), dma(()),
            dma(()), dma((2, 4)),
            dma((6,)), dma((4, 2)),
            dma(()), dma(()),
            dma((ROUNDS,)), dma((ROUNDS, 2)),
        ],
        compiler_params=pltpu.CompilerParams(
            collective_id=0, has_side_effects=True, vmem_limit_bytes=VMEM_LIMIT
        ),
        cost_estimate=pl.CostEstimate(flops=15 << 30, bytes_accessed=8 << 20, transcendentals=0),
    )(
        tensor.reshape(S, PL, NB, S), tensor_mask,
        occ_density.reshape(S, 2, S), occ_mask, virt_density.reshape(S, 2, S), virt_mask,
    )
    out = pl.pallas_call(
        last_kernel,
        out_shape=jax.ShapeDtypeStruct((NB * S, PL, S), BF16),
        in_specs=[vmem] * 3,
        out_specs=pl.BlockSpec(memory_space=pl.ANY),
        scratch_shapes=[pltpu.VMEM((NB * S, PL, S), BF16), dma(())],
        compiler_params=pltpu.CompilerParams(vmem_limit_bytes=LAST_LIMIT),
        cost_estimate=pl.CostEstimate(flops=2 << 30, bytes_accessed=4 << 20, transcendentals=0),
    )(virt, recv, done)
    return out.reshape(NB, S, PL, 1, S)


def solution(mesh):
    placed = (
        P("wide", None, "narrow", None, None),
        P("wide", None),
        P("wide", None, "narrow", None),
        P("wide", "narrow"),
        P("wide", None, "narrow", None),
        P("wide", "narrow"),
    )
    return jax.shard_map(
        shards,
        mesh=mesh,
        in_specs=placed,
        out_specs=P(None, None, "narrow", "wide", None),
        check_vma=False,
    )
```

```python
import functools

import jax
import jax.numpy as jnp
from jax import lax
from jax.experimental import pallas as pl
from jax.experimental.pallas import tpu as pltpu
from jax.sharding import PartitionSpec as P

MESH = pl.DeviceIdType.MESH
BF16 = jnp.bfloat16
F32 = jnp.float32
S = 128
NB = 16
PL = 8
ROUNDS = 4
ROWS = 2 * PL * S
NA = 80
NC = S - NA
VMEM_LIMIT = 47 << 20
LAST_LIMIT = 8 << 20
AHEAD = 2
CHUNK = 4 * S
HALF = NB * S // 2


NEAR = (
    (1, 0), (0, 1), (3, 0), (0, 3), (1, 1), (3, 3), (1, 3), (3, 1),
    (2, 0), (0, 2), (2, 1), (1, 2), (2, 3), (3, 2), (2, 2),
)


def ring(v):
    return lax.rem(v + 4, 4)


def chunk_rows(m):
    return pl.ds(pl.multiple_of(m * CHUNK, CHUNK), CHUNK)


def product(virt, recv, r, m):
    lhs = virt[m].reshape(CHUNK, NB * S)
    return jnp.dot(lhs, recv[r], preferred_element_type=F32).astype(BF16).reshape(CHUNK, 2, S)


def last_kernel(virt, recv, done, out_hbm, outv, out_sem):
    def body(m, c):
        rows = chunk_rows(m)
        outv[rows] = done[rows]
        outv[rows, PL - 2 : PL, :] = product(virt, recv, ROUNDS - 1, m)
        pltpu.make_async_copy(outv.at[rows], out_hbm.at[rows], out_sem).start()
        return c

    lax.fori_loop(0, NB * S // CHUNK, body, 0)
    pltpu.make_async_copy(outv, out_hbm, out_sem).wait()


def kernel(
    t_hbm, tmask_hbm, occ_hbm, omask_hbm, virt_hbm, vmask_hbm, virt, recv, done,
    tmask, occ_ref, omask, virt_ref, vmask, in_sem, traw, tm, occ, send, perm, early,
    t_sem, x_ssem, x_rsem, o1_ssem, o1_rsem, o2_ssem, o3_ssem, o_rsem, c1_ssem, c1_rsem, c2_ssem, c2_rsem,
    v1_ssem, v1_rsem, v1b_ssem, v1b_rsem, v2_ssem, v2_rsem, v3_ssem, v3_rsem,
    a_ssem, a_rsem,
):
    w = lax.axis_index("wide")
    n = lax.axis_index("narrow")
    x, z = w // 4, lax.rem(w, 4)
    y, k = n // 2, lax.rem(n, 2)

    def remote(src, dst, ssem, rsem, wide, narrow):
        return pltpu.make_async_remote_copy(
            src_ref=src, dst_ref=dst, send_sem=ssem, recv_sem=rsem,
            device_id=(wide, narrow), device_id_type=MESH,
        )

    def wait_kib(sem, kib):
        view = recv.at[0, pl.ds(0, kib * 2), :] if kib < 1024 else tm.at[pl.ds(0, kib // 4), :]
        pltpu.make_async_copy(view, view, sem).wait()

    barrier = pltpu.get_barrier_semaphore()
    for dx, dz in reversed(NEAR):
        for e in range(2):
            pl.semaphore_signal(
                barrier,
                inc=1,
                device_id=(ring(x + dx) * 4 + ring(z + dz), y * 2 + e),
                device_id_type=MESH,
            )
    for d in (2, 1, 3):
        pl.semaphore_signal(barrier, inc=1, device_id=(w, ring(y + d) * 2 + k), device_id_type=MESH)
    pl.semaphore_signal(barrier, inc=1, device_id=(w, y * 2 + 1 - k), device_id_type=MESH)

    inputs = [
        pltpu.make_async_copy(src, dst, in_sem.at[t])
        for t, (src, dst) in enumerate(
            (
                (omask_hbm, omask), (occ_hbm, occ_ref), (vmask_hbm, vmask),
                (virt_hbm, virt_ref), (tmask_hbm, tmask),
            )
        )
    ]
    for copy in inputs:
        copy.start()
    for p in range(PL):
        pltpu.make_async_copy(t_hbm.at[:, p], traw.at[p], t_sem.at[p]).start()
    inputs[0].wait()
    inputs[1].wait()

    ycol = pl.ds(pl.multiple_of(y * S, S), S)
    ncol = pl.ds(pl.multiple_of(n * 2 * S, 2 * S), 2 * S)
    wrow = pl.ds(pl.multiple_of(w * S, S), S)
    for j in range(2):
        block = occ_ref[:, j, :].astype(F32) * omask[0, j].astype(F32)
        occ[j, w, :, ycol] = block.astype(BF16)
    pl.semaphore_wait(barrier, 34)

    first, other = pl.ds(0, NA), pl.ds(NA, NC)
    for d in (1, 3, 2):
        for i in range(2):
            own = occ.at[i, w, first, ycol]
            remote(own, own, o1_ssem, o1_rsem, w, ring(y + d) * 2 + k).start()
    for dx, dz in NEAR:
        own = occ.at[:, w, other, ycol]
        remote(own, own, c1_ssem, c1_rsem, ring(x + dx) * 4 + ring(z + dz), n).start()
    place = ((x, z), (z, x))

    def at(i, p, q):
        return p * 4 + q if i == 0 else q * 4 + p

    upper, lower = pl.ds(0, S // 2), pl.ds(S // 2, S // 2)
    def own_rows(r):
        return pl.ds(pl.multiple_of(r * 512 + k * 256, 256), 256)

    def relayout(r):
        for pi in range(2):
            p = 2 * r + pi
            pltpu.make_async_copy(t_hbm.at[:, p], traw.at[p], t_sem.at[p]).wait()

            def body(g, c, p=p, pi=pi):
                pair = jnp.concatenate(
                    [
                        traw[p, pl.ds(pl.multiple_of(g * 32 + h * 16, 16), 16)].reshape(256, S)
                        for h in range(2)
                    ],
                    axis=1,
                )
                got = jnp.dot(perm[...], pair, preferred_element_type=F32).astype(BF16)
                for h in range(2):
                    top = r * 512 + k * 256 + pi * S + g * 32 + h * 16
                    for b in range(NB):
                        tm[pl.ds(pl.multiple_of(top, 16), 16), b * S : (b + 1) * S] = got[
                            b * 16 : (b + 1) * 16, h * S : (h + 1) * S
                        ]
                return c

            lax.fori_loop(0, 4, body, 0)
        mine = tm.at[own_rows(r), :]
        remote(mine, mine, x_ssem.at[r], x_rsem.at[r], w, y * 2 + 1 - k).start()

    def pass_block(i, b, p, q, ssem=o3_ssem):
        part = occ.at[i, b, first, :]
        remote(part, part, ssem, o_rsem.at[i, b], at(i, p, q), n).start()

    def wait_block(i, b):
        part = occ.at[i, b, first, :]
        pltpu.make_async_copy(part, part, o_rsem.at[i, b]).wait()

    def spread(i, yy, d):
        part = occ.at[i, :, other, pl.ds(pl.multiple_of(yy * S, S), S)]
        remote(part, part, c2_ssem, c2_rsem.at[yy, i], w, ring(y + d) * 2 + k).start()

    def wait_spread(i, yy):
        part = occ.at[i, :, other, pl.ds(pl.multiple_of(yy * S, S), S)]
        pltpu.make_async_copy(part, part, c2_rsem.at[yy, i]).wait()

    up, down, far = ring(y + 1), ring(y + 3), ring(y + 2)

    wait_kib(o1_rsem, 6 * NA // 4)
    for d in (1, 3, 2):
        for i in range(2):
            p, q = place[i]
            pass_block(i, w, ring(p + d), q, o2_ssem)
    for i in range(2):
        p, q = place[i]
        for d in (1, 3):
            pass_block(i, w, p, ring(q + d))

    wait_kib(c1_rsem, 15 * NC // 2)
    for i, d in ((0, 3), (1, 1), (0, 1), (1, 3)):
        spread(i, y, d)
    inputs[2].wait()
    inputs[3].wait()
    for j in range(2):
        block = virt_ref[:, j, :].astype(F32) * vmask[0, j].astype(F32)
        virt[x, z, :, pl.ds(pl.multiple_of(n * 2 * S + j * S, S), S)] = block.astype(BF16)
    for d in (1, 3, 2):
        for i, part in enumerate((upper, lower)):
            p, q = place[i]
            own = virt.at[x, z, part, ncol]
            remote(own, own, v1_ssem, v1_rsem, at(i, ring(p + d), q), n).start()

    inputs[4].wait()
    row = lax.broadcasted_iota(jnp.int32, (256, 256), 0)
    col = lax.broadcasted_iota(jnp.int32, (256, 256), 1)
    scale = jnp.zeros((256, 256), F32)
    for b in range(NB):
        scale = scale + jnp.where((row >> 4) == b, 1.0, 0.0) * tmask[0, b].astype(F32)
    hit = jnp.logical_and((row >> 4) == (col & 15), (row & 15) == (col >> 4))
    perm[...] = jnp.where(hit, scale, 0.0).astype(BF16)

    relayout(0)
    for d in (1, 3, 2):
        for i in range(2):
            p, q = place[i]
            b = at(i, ring(p + d), q)
            wait_block(i, b)
            for f in (1, 3):
                pass_block(i, b, p, ring(q + f))
    def line(i, q, h=None):
        part = pl.ds(0, 4) if h is None else pl.ds(2 * h, 2)
        return virt.at[part, q, upper, ncol] if i == 0 else virt.at[q, part, lower, ncol]

    def pass_line(i, q, d, t, h=None):
        ref = line(i, q, h)
        p, here = place[i]
        remote(ref, ref, v1b_ssem, v1b_rsem.at[i, t], at(i, p, ring(here + d)), n).start()

    def wait_line(i, q, t, h=None):
        ref = line(i, q, h)
        pltpu.make_async_copy(ref, ref, v1b_rsem.at[i, t]).wait()

    wait_kib(v1_rsem, 192)
    for i in range(2):
        q = place[i][1]
        pass_line(i, q, 3, 0)
        pass_line(i, q, 1, 1)

    relayout(1)
    wait_spread(0, up)
    spread(0, up, 3)
    wait_spread(1, down)
    spread(1, down, 1)
    for f, g in ((0, 3), (1, 2)):
        for i in range(2):
            p, q = place[i]
            for dq, dp, to in ((1, f, 3), (3, g, 1)):
                b = at(i, ring(p + dp), ring(q + dq))
                wait_block(i, b)
                pass_block(i, b, p, ring(q + to))

    halves = [pl.ds(0, 2), pl.ds(2, 2)]

    def columns(yy, kk):
        return pl.ds(pl.multiple_of((yy * 2 + kk) * 2 * S, 2 * S), 2 * S)

    def to_core(yy, h, t=0):
        part = virt.at[halves[h], :, :, columns(yy, k)]
        remote(part, part, v3_ssem, v3_rsem.at[t], w, y * 2 + 1 - k).start()

    def along(yy, h, d, s):
        part = virt.at[halves[h], :, :, columns(yy, k)]
        remote(part, part, v2_ssem.at[s], v2_rsem.at[lax.rem(yy, 4), h], w, ring(y + d) * 2 + k).start()

    def wait_along(yy, h):
        part = virt.at[halves[h], :, :, columns(yy, k)]
        pltpu.make_async_copy(part, part, v2_rsem.at[yy, h]).wait()

    for i in range(2):
        q = place[i][1]
        wait_line(i, ring(q + 1), 0)
        pass_line(i, ring(q + 1), 3, 2, 0)
        wait_line(i, ring(q + 3), 1)
        pass_line(i, ring(q + 3), 1, 3, 1)
    relayout(2)
    relayout(3)
    for i in range(2):
        p, q = place[i]
        for dq, dp in ((1, 3), (1, 2), (3, 0), (3, 1), (2, 0), (2, 1), (2, 2), (2, 3)):
            wait_block(i, at(i, ring(p + dp), ring(q + dq)))
        for yy in (far, up if i == 1 else down):
            wait_spread(i, yy)

    def first_product(r, c):
        theirs = tm.at[pl.ds(pl.multiple_of(r * 512 + (1 - k) * 256, 256), 256), :]
        pltpu.make_async_copy(theirs, theirs, x_rsem.at[r]).wait()
        for j in range(2):
            i = lax.rem(j + x // 2, 2)
            for e in range(2):
                rows = pl.ds(pl.multiple_of(r * 512 + e * 256, 256), 256)
                got = jnp.dot(
                    tm[rows, :], occ[i].reshape(NB * S, 4 * S), preferred_element_type=F32
                ).astype(BF16)
                for xx in range(4):
                    for pi in range(2):
                        send[r, i, xx, e, :, pi * S : (pi + 1) * S] = got[
                            pi * S : (pi + 1) * S, xx * S : (xx + 1) * S
                        ]
                for d in (1, 3, 2, 0):
                    xx = ring(x + d)
                    wide = xx * 4 + 2 * k + i
                    here = jnp.logical_and(wide == w, k == e)
                    src = send.at[r, i, xx, e]
                    dst = recv.at[r, wrow, :]
                    rsem = a_rsem.at[r, x // 2]

                    def away(src=src, dst=dst, rsem=rsem, wide=wide, e=e):
                        remote(src, dst, a_ssem.at[r], rsem, wide, y * 2 + e).start()

                    if d == 0:
                        pl.when(jnp.logical_not(here))(away)

                        @pl.when(here)
                        def _(src=src, dst=dst, rsem=rsem):
                            pltpu.make_async_copy(src, dst, rsem).start()
                    else:
                        away()
        return c

    first_product(0, 0)
    for i in range(2):
        q = place[i][1]
        for h in range(2):
            wait_line(i, ring(q + 2), 2 + h, h)
    along(y, 0, 3, 0)
    along(y, 1, 1, 1)
    along(y, 1, 3, 2)
    along(y, 0, 1, 3)
    to_core(y, 0)
    to_core(y, 1)

    lax.fori_loop(1, ROUNDS, first_product, 0)

    wait_along(up, 0)
    along(up, 0, 3, 4)
    to_core(up, 0)
    wait_along(down, 1)
    along(down, 1, 1, 5)
    to_core(down, 1)
    wait_along(up, 1)
    to_core(up, 1)
    wait_along(down, 0)
    to_core(down, 0)
    def arrive(r, h):
        half = recv.at[r, pl.ds(pl.multiple_of(h * HALF, HALF), HALF), :]
        pltpu.make_async_copy(half, half, a_rsem.at[r, h]).wait()

    def some(r, m, planes):
        cols = [pl.ds(pl.multiple_of(yy * 4 * S, 4 * S), 4 * S) for yy in planes]
        lhs = jnp.concatenate([virt[m, :, :, c].reshape(CHUNK, 4 * S) for c in cols], axis=1)
        rhs = jnp.concatenate([recv[r, c, :] for c in cols], axis=0)
        return jnp.dot(lhs, rhs, preferred_element_type=F32)

    wait_kib(v3_rsem.at[0], 3072)
    for r in range(AHEAD):
        arrive(r, 0)
        arrive(r, 1)

        def begin(m, c, r=r):
            early[r, chunk_rows(m), :] = some(r, m, (y, up, down))
            return c

        lax.fori_loop(0, NB * S // CHUNK, begin, 0)

    for h in range(2):
        wait_along(far, h)
        to_core(far, h, 1)
    wait_kib(v3_rsem.at[1], 1024)

    for r in range(ROUNDS - 1):
        if r >= AHEAD:
            arrive(r, 0)
            arrive(r, 1)

        def second_product(m, c, r=r):
            rows = chunk_rows(m)
            if r < AHEAD:
                got = (early[r, rows, :] + some(r, m, (far,))).astype(BF16).reshape(CHUNK, 2, S)
            else:
                got = product(virt, recv, r, m)
            done[rows, 2 * r : 2 * r + 2, :] = got
            return c

        lax.fori_loop(0, NB * S // CHUNK, second_product, 0)

    def wait_sent(r):
        local = z // 2 == k

        @pl.when(local)
        def _():
            wait_kib(a_ssem.at[r], 960)

        @pl.when(jnp.logical_not(local))
        def _():
            wait_kib(a_ssem.at[r], 1024)

    wait_kib(o1_ssem, 6 * NA // 4)
    wait_kib(o2_ssem, 6 * NA)
    wait_kib(o3_ssem, 24 * NA)
    wait_kib(c1_ssem, 15 * NC // 2)
    wait_kib(c2_ssem, 24 * NC)
    wait_kib(v1_ssem, 192)
    wait_kib(v1b_ssem, 768)
    for t in range(6):
        wait_kib(v2_ssem.at[t], 512)
    wait_kib(v3_ssem, 4096)
    for r in range(ROUNDS):
        mine = tm.at[own_rows(r), :]
        pltpu.make_async_copy(mine, mine, x_ssem.at[r]).wait()
        if r < ROUNDS - 1:
            wait_sent(r)

    arrive(ROUNDS - 1, 0)
    arrive(ROUNDS - 1, 1)
    wait_sent(ROUNDS - 1)


def shards(tensor, tensor_mask, occ_density, occ_mask, virt_density, virt_mask):
    dma = pltpu.SemaphoreType.DMA
    vmem, hbm = pl.BlockSpec(memory_space=pltpu.VMEM), pl.BlockSpec(memory_space=pl.ANY)
    virt, recv, done = pl.pallas_call(
        kernel,
        out_shape=[
            pltpu.VMEM((4, 4, S, NB * S), BF16),
            pltpu.VMEM((ROUNDS, NB * S, 2 * S), BF16),
            pltpu.VMEM((NB * S, PL, S), BF16),
        ],
        in_specs=[hbm] * 6,
        out_specs=[vmem] * 3,
        scratch_shapes=[
            pltpu.SMEM((1, NB), jnp.int32),
            pltpu.VMEM((S, 2, S), BF16),
            pltpu.SMEM((1, 2), jnp.int32),
            pltpu.VMEM((S, 2, S), BF16),
            pltpu.SMEM((1, 2), jnp.int32),
            dma((5,)),
            pltpu.VMEM((PL, S, NB, S), BF16),
            pltpu.VMEM((ROWS, NB * S), BF16),
            pltpu.VMEM((2, NB, S, 4 * S), BF16),
            pltpu.VMEM((ROUNDS, 2, 4, 2, S, 2 * S), BF16),
            pltpu.VMEM((256, 256), BF16),
            pltpu.VMEM((AHEAD, NB * S, 2 * S), F32),
            dma((PL,)),
            dma((ROUNDS,)), dma((ROUNDS,)),
            dma(()), dma(()),
            dma(()), dma(()), dma((2, NB)),
            dma(()), dma(()), dma(()), dma((4, 2)),
            dma(()), dma(()),
            dma(()), dma((2, 4)),
            dma((6,)), dma((4, 2)),
            dma(()), dma((2,)),
            dma((ROUNDS,)), dma((ROUNDS, 2)),
        ],
        compiler_params=pltpu.CompilerParams(
            collective_id=0, has_side_effects=True, vmem_limit_bytes=VMEM_LIMIT
        ),
        cost_estimate=pl.CostEstimate(flops=15 << 30, bytes_accessed=8 << 20, transcendentals=0),
    )(
        tensor.reshape(S, PL, NB, S), tensor_mask,
        occ_density.reshape(S, 2, S), occ_mask, virt_density.reshape(S, 2, S), virt_mask,
    )
    out = pl.pallas_call(
        last_kernel,
        out_shape=jax.ShapeDtypeStruct((NB * S, PL, S), BF16),
        in_specs=[vmem] * 3,
        out_specs=pl.BlockSpec(memory_space=pl.ANY),
        scratch_shapes=[pltpu.VMEM((NB * S, PL, S), BF16), dma(())],
        compiler_params=pltpu.CompilerParams(vmem_limit_bytes=LAST_LIMIT),
        cost_estimate=pl.CostEstimate(flops=2 << 30, bytes_accessed=4 << 20, transcendentals=0),
    )(virt, recv, done)
    return out.reshape(NB, S, PL, 1, S)


def solution(mesh):
    placed = (
        P("wide", None, "narrow", None, None),
        P("wide", None),
        P("wide", None, "narrow", None),
        P("wide", "narrow"),
        P("wide", None, "narrow", None),
        P("wide", "narrow"),
    )
    return jax.shard_map(
        shards,
        mesh=mesh,
        in_specs=placed,
        out_specs=P(None, None, "narrow", "wide", None),
        check_vma=False,
    )
```

```python
import functools

import jax
import jax.numpy as jnp
from jax import lax
from jax.experimental import pallas as pl
from jax.experimental.pallas import tpu as pltpu
from jax.sharding import PartitionSpec as P

MESH = pl.DeviceIdType.MESH
BF16 = jnp.bfloat16
F32 = jnp.float32
S = 128
NB = 16
PL = 8
ROUNDS = 4
ROWS = 2 * PL * S
NA = 80
NC = S - NA
VMEM_LIMIT = 47 << 20
LAST_LIMIT = 8 << 20
AHEAD = 2
CHUNK = 4 * S
HALF = NB * S // 2


NEAR = (
    (1, 0), (0, 1), (3, 0), (0, 3), (1, 1), (3, 3), (1, 3), (3, 1),
    (2, 0), (0, 2), (2, 1), (1, 2), (2, 3), (3, 2), (2, 2),
)


def ring(v):
    return lax.rem(v + 4, 4)


def chunk_rows(m):
    return pl.ds(pl.multiple_of(m * CHUNK, CHUNK), CHUNK)


def product(virt, recv, r, m):
    lhs = virt[m].reshape(CHUNK, NB * S)
    return jnp.dot(lhs, recv[r], preferred_element_type=F32).astype(BF16).reshape(CHUNK, 2, S)


def last_kernel(virt, recv, done, out_hbm, outv, out_sem):
    def body(m, c):
        rows = chunk_rows(m)
        outv[rows] = done[rows]
        outv[rows, PL - 2 : PL, :] = product(virt, recv, ROUNDS - 1, m)
        pltpu.make_async_copy(outv.at[rows], out_hbm.at[rows], out_sem).start()
        return c

    lax.fori_loop(0, NB * S // CHUNK, body, 0)
    pltpu.make_async_copy(outv, out_hbm, out_sem).wait()


def kernel(
    t_hbm, tmask_hbm, occ_hbm, omask_hbm, virt_hbm, vmask_hbm, virt, recv, done,
    tmask, occ_ref, omask, virt_ref, vmask, in_sem, traw, tm, occ, send, perm, early,
    t_sem, x_ssem, x_rsem, o1_ssem, o1_rsem, o2_ssem, o3_ssem, o_rsem, c1_ssem, c1_rsem, c2_ssem, c2_rsem,
    v1_ssem, v1_rsem, v1b_ssem, v1b_rsem, v2_ssem, v2_rsem, v3_ssem, v3_rsem,
    a_ssem, a_rsem,
):
    w = lax.axis_index("wide")
    n = lax.axis_index("narrow")
    x, z = w // 4, lax.rem(w, 4)
    y, k = n // 2, lax.rem(n, 2)

    def remote(src, dst, ssem, rsem, wide, narrow):
        return pltpu.make_async_remote_copy(
            src_ref=src, dst_ref=dst, send_sem=ssem, recv_sem=rsem,
            device_id=(wide, narrow), device_id_type=MESH,
        )

    def wait_kib(sem, kib):
        view = recv.at[0, pl.ds(0, kib * 2), :] if kib < 1024 else tm.at[pl.ds(0, kib // 4), :]
        pltpu.make_async_copy(view, view, sem).wait()

    barrier = pltpu.get_barrier_semaphore()
    for dx, dz in reversed(NEAR):
        for e in range(2):
            pl.semaphore_signal(
                barrier,
                inc=1,
                device_id=(ring(x + dx) * 4 + ring(z + dz), y * 2 + e),
                device_id_type=MESH,
            )
    for d in (2, 1, 3):
        pl.semaphore_signal(barrier, inc=1, device_id=(w, ring(y + d) * 2 + k), device_id_type=MESH)
    pl.semaphore_signal(barrier, inc=1, device_id=(w, y * 2 + 1 - k), device_id_type=MESH)

    inputs = [
        pltpu.make_async_copy(src, dst, in_sem.at[t])
        for t, (src, dst) in enumerate(
            (
                (omask_hbm, omask), (occ_hbm, occ_ref), (vmask_hbm, vmask),
                (virt_hbm, virt_ref), (tmask_hbm, tmask),
            )
        )
    ]
    for copy in inputs:
        copy.start()
    for p in range(PL):
        pltpu.make_async_copy(t_hbm.at[:, p], traw.at[p], t_sem.at[p]).start()
    inputs[0].wait()
    inputs[1].wait()

    ycol = pl.ds(pl.multiple_of(y * S, S), S)
    ncol = pl.ds(pl.multiple_of(n * 2 * S, 2 * S), 2 * S)
    wrow = pl.ds(pl.multiple_of(w * S, S), S)
    for j in range(2):
        block = occ_ref[:, j, :].astype(F32) * omask[0, j].astype(F32)
        occ[j, w, :, ycol] = block.astype(BF16)
    pl.semaphore_wait(barrier, 34)

    first, other = pl.ds(0, NA), pl.ds(NA, NC)
    for d in (1, 3, 2):
        for i in range(2):
            own = occ.at[i, w, first, ycol]
            remote(own, own, o1_ssem, o1_rsem, w, ring(y + d) * 2 + k).start()
    for dx, dz in NEAR:
        own = occ.at[:, w, other, ycol]
        remote(own, own, c1_ssem, c1_rsem, ring(x + dx) * 4 + ring(z + dz), n).start()
    place = ((x, z), (z, x))

    def at(i, p, q):
        return p * 4 + q if i == 0 else q * 4 + p

    upper, lower = pl.ds(0, S // 2), pl.ds(S // 2, S // 2)
    def own_rows(r):
        return pl.ds(pl.multiple_of(r * 512 + k * 256, 256), 256)

    def relayout(r):
        for pi in range(2):
            p = 2 * r + pi
            pltpu.make_async_copy(t_hbm.at[:, p], traw.at[p], t_sem.at[p]).wait()

            def body(g, c, p=p, pi=pi):
                pair = jnp.concatenate(
                    [
                        traw[p, pl.ds(pl.multiple_of(g * 32 + h * 16, 16), 16)].reshape(256, S)
                        for h in range(2)
                    ],
                    axis=1,
                )
                got = jnp.dot(perm[...], pair, preferred_element_type=F32).astype(BF16)
                for h in range(2):
                    top = r * 512 + k * 256 + pi * S + g * 32 + h * 16
                    for b in range(NB):
                        tm[pl.ds(pl.multiple_of(top, 16), 16), b * S : (b + 1) * S] = got[
                            b * 16 : (b + 1) * 16, h * S : (h + 1) * S
                        ]
                return c

            lax.fori_loop(0, 4, body, 0)
        mine = tm.at[own_rows(r), :]
        remote(mine, mine, x_ssem.at[r], x_rsem.at[r], w, y * 2 + 1 - k).start()

    def pass_block(i, b, p, q, ssem=o3_ssem):
        part = occ.at[i, b, first, :]
        remote(part, part, ssem, o_rsem.at[i, b], at(i, p, q), n).start()

    def wait_block(i, b):
        part = occ.at[i, b, first, :]
        pltpu.make_async_copy(part, part, o_rsem.at[i, b]).wait()

    def spread(i, yy, d):
        part = occ.at[i, :, other, pl.ds(pl.multiple_of(yy * S, S), S)]
        remote(part, part, c2_ssem, c2_rsem.at[yy, i], w, ring(y + d) * 2 + k).start()

    def wait_spread(i, yy):
        part = occ.at[i, :, other, pl.ds(pl.multiple_of(yy * S, S), S)]
        pltpu.make_async_copy(part, part, c2_rsem.at[yy, i]).wait()

    up, down, far = ring(y + 1), ring(y + 3), ring(y + 2)

    wait_kib(o1_rsem, 6 * NA // 4)
    for d in (1, 3, 2):
        for i in range(2):
            p, q = place[i]
            pass_block(i, w, ring(p + d), q, o2_ssem)
    for i in range(2):
        p, q = place[i]
        for d in (1, 3):
            pass_block(i, w, p, ring(q + d))

    wait_kib(c1_rsem, 15 * NC // 2)
    for i, d in ((0, 3), (1, 1), (0, 1), (1, 3)):
        spread(i, y, d)
    inputs[2].wait()
    inputs[3].wait()
    for j in range(2):
        block = virt_ref[:, j, :].astype(F32) * vmask[0, j].astype(F32)
        virt[x, z, :, pl.ds(pl.multiple_of(n * 2 * S + j * S, S), S)] = block.astype(BF16)
    for d in (1, 3, 2):
        for i, part in enumerate((upper, lower)):
            p, q = place[i]
            own = virt.at[x, z, part, ncol]
            remote(own, own, v1_ssem, v1_rsem, at(i, ring(p + d), q), n).start()

    inputs[4].wait()
    row = lax.broadcasted_iota(jnp.int32, (256, 256), 0)
    col = lax.broadcasted_iota(jnp.int32, (256, 256), 1)
    scale = jnp.zeros((256, 256), F32)
    for b in range(NB):
        scale = scale + jnp.where((row >> 4) == b, 1.0, 0.0) * tmask[0, b].astype(F32)
    hit = jnp.logical_and((row >> 4) == (col & 15), (row & 15) == (col >> 4))
    perm[...] = jnp.where(hit, scale, 0.0).astype(BF16)

    relayout(0)
    for d in (1, 3, 2):
        for i in range(2):
            p, q = place[i]
            b = at(i, ring(p + d), q)
            wait_block(i, b)
            for f in (1, 3):
                pass_block(i, b, p, ring(q + f))
    def line(i, q, h=None):
        part = pl.ds(0, 4) if h is None else pl.ds(2 * h, 2)
        return virt.at[part, q, upper, ncol] if i == 0 else virt.at[q, part, lower, ncol]

    def pass_line(i, q, d, t, h=None):
        ref = line(i, q, h)
        p, here = place[i]
        remote(ref, ref, v1b_ssem, v1b_rsem.at[i, t], at(i, p, ring(here + d)), n).start()

    def wait_line(i, q, t, h=None):
        ref = line(i, q, h)
        pltpu.make_async_copy(ref, ref, v1b_rsem.at[i, t]).wait()

    wait_kib(v1_rsem, 192)
    for i in range(2):
        q = place[i][1]
        pass_line(i, q, 3, 0)
        pass_line(i, q, 1, 1)

    relayout(1)
    wait_spread(0, up)
    spread(0, up, 3)
    wait_spread(1, down)
    spread(1, down, 1)
    for f, g in ((0, 3), (1, 2)):
        for i in range(2):
            p, q = place[i]
            for dq, dp, to in ((1, f, 3), (3, g, 1)):
                b = at(i, ring(p + dp), ring(q + dq))
                wait_block(i, b)
                pass_block(i, b, p, ring(q + to))

    halves = [pl.ds(0, 2), pl.ds(2, 2)]

    def columns(yy, kk):
        return pl.ds(pl.multiple_of((yy * 2 + kk) * 2 * S, 2 * S), 2 * S)

    def to_core(yy, h, t=0):
        part = virt.at[halves[h], :, :, columns(yy, k)]
        remote(part, part, v3_ssem, v3_rsem.at[t], w, y * 2 + 1 - k).start()

    def along(yy, h, d, s):
        part = virt.at[halves[h], :, :, columns(yy, k)]
        remote(part, part, v2_ssem.at[s], v2_rsem.at[lax.rem(yy, 4), h], w, ring(y + d) * 2 + k).start()

    def wait_along(yy, h):
        part = virt.at[halves[h], :, :, columns(yy, k)]
        pltpu.make_async_copy(part, part, v2_rsem.at[yy, h]).wait()

    for i in range(2):
        q = place[i][1]
        wait_line(i, ring(q + 1), 0)
        pass_line(i, ring(q + 1), 3, 2, 0)
        wait_line(i, ring(q + 3), 1)
        pass_line(i, ring(q + 3), 1, 3, 1)
    relayout(2)
    relayout(3)
    for i in range(2):
        p, q = place[i]
        for dq, dp in ((1, 3), (1, 2), (3, 0), (3, 1), (2, 0), (2, 1), (2, 2), (2, 3)):
            wait_block(i, at(i, ring(p + dp), ring(q + dq)))
        for yy in (far, up if i == 1 else down):
            wait_spread(i, yy)

    def virt_along():
        for i in range(2):
            q = place[i][1]
            for h in range(2):
                wait_line(i, ring(q + 2), 2 + h, h)
        along(y, 0, 3, 0)
        along(y, 1, 1, 1)
        along(y, 1, 3, 2)
        along(y, 0, 1, 3)
        to_core(y, 0)
        to_core(y, 1)

    def first_product(r, c):
        theirs = tm.at[pl.ds(pl.multiple_of(r * 512 + (1 - k) * 256, 256), 256), :]
        pltpu.make_async_copy(theirs, theirs, x_rsem.at[r]).wait()
        for j in range(2):
            i = lax.rem(j + x // 2, 2)
            for e in range(2):
                rows = pl.ds(pl.multiple_of(r * 512 + e * 256, 256), 256)
                got = jnp.dot(
                    tm[rows, :], occ[i].reshape(NB * S, 4 * S), preferred_element_type=F32
                ).astype(BF16)
                for xx in range(4):
                    for pi in range(2):
                        send[r, i, xx, e, :, pi * S : (pi + 1) * S] = got[
                            pi * S : (pi + 1) * S, xx * S : (xx + 1) * S
                        ]
                for d in (1, 3, 2, 0):
                    xx = ring(x + d)
                    wide = xx * 4 + 2 * k + i
                    here = jnp.logical_and(wide == w, k == e)
                    src = send.at[r, i, xx, e]
                    dst = recv.at[r, wrow, :]
                    rsem = a_rsem.at[r, x // 2]

                    def away(src=src, dst=dst, rsem=rsem, wide=wide, e=e):
                        remote(src, dst, a_ssem.at[r], rsem, wide, y * 2 + e).start()

                    if d == 0:
                        pl.when(jnp.logical_not(here))(away)

                        @pl.when(here)
                        def _(src=src, dst=dst, rsem=rsem):
                            pltpu.make_async_copy(src, dst, rsem).start()
                    else:
                        away()
            if j == 0 and isinstance(r, int):
                virt_along()
        return c

    first_product(0, 0)
    lax.fori_loop(1, ROUNDS, first_product, 0)

    wait_along(up, 0)
    along(up, 0, 3, 4)
    to_core(up, 0)
    wait_along(down, 1)
    along(down, 1, 1, 5)
    to_core(down, 1)
    wait_along(up, 1)
    to_core(up, 1)
    wait_along(down, 0)
    to_core(down, 0)
    def arrive(r, h):
        half = recv.at[r, pl.ds(pl.multiple_of(h * HALF, HALF), HALF), :]
        pltpu.make_async_copy(half, half, a_rsem.at[r, h]).wait()

    def some(r, m, planes):
        cols = [pl.ds(pl.multiple_of(yy * 4 * S, 4 * S), 4 * S) for yy in planes]
        lhs = jnp.concatenate([virt[m, :, :, c].reshape(CHUNK, 4 * S) for c in cols], axis=1)
        rhs = jnp.concatenate([recv[r, c, :] for c in cols], axis=0)
        return jnp.dot(lhs, rhs, preferred_element_type=F32)

    wait_kib(v3_rsem.at[0], 3072)
    for r in range(AHEAD):
        arrive(r, 0)
        arrive(r, 1)

        def begin(m, c, r=r):
            early[r, chunk_rows(m), :] = some(r, m, (y, up, down))
            return c

        lax.fori_loop(0, NB * S // CHUNK, begin, 0)

    for h in range(2):
        wait_along(far, h)
        to_core(far, h, 1)
    wait_kib(v3_rsem.at[1], 1024)

    for r in range(ROUNDS - 1):
        if r >= AHEAD:
            arrive(r, 0)
            arrive(r, 1)

        def second_product(m, c, r=r):
            rows = chunk_rows(m)
            if r < AHEAD:
                got = (early[r, rows, :] + some(r, m, (far,))).astype(BF16).reshape(CHUNK, 2, S)
            else:
                got = product(virt, recv, r, m)
            done[rows, 2 * r : 2 * r + 2, :] = got
            return c

        lax.fori_loop(0, NB * S // CHUNK, second_product, 0)

    def wait_sent(r):
        local = z // 2 == k

        @pl.when(local)
        def _():
            wait_kib(a_ssem.at[r], 960)

        @pl.when(jnp.logical_not(local))
        def _():
            wait_kib(a_ssem.at[r], 1024)

    wait_kib(o1_ssem, 6 * NA // 4)
    wait_kib(o2_ssem, 6 * NA)
    wait_kib(o3_ssem, 24 * NA)
    wait_kib(c1_ssem, 15 * NC // 2)
    wait_kib(c2_ssem, 24 * NC)
    wait_kib(v1_ssem, 192)
    wait_kib(v1b_ssem, 768)
    for t in range(6):
        wait_kib(v2_ssem.at[t], 512)
    wait_kib(v3_ssem, 4096)
    for r in range(ROUNDS):
        mine = tm.at[own_rows(r), :]
        pltpu.make_async_copy(mine, mine, x_ssem.at[r]).wait()
        if r < ROUNDS - 1:
            wait_sent(r)

    arrive(ROUNDS - 1, 0)
    arrive(ROUNDS - 1, 1)
    wait_sent(ROUNDS - 1)


def shards(tensor, tensor_mask, occ_density, occ_mask, virt_density, virt_mask):
    dma = pltpu.SemaphoreType.DMA
    vmem, hbm = pl.BlockSpec(memory_space=pltpu.VMEM), pl.BlockSpec(memory_space=pl.ANY)
    virt, recv, done = pl.pallas_call(
        kernel,
        out_shape=[
            pltpu.VMEM((4, 4, S, NB * S), BF16),
            pltpu.VMEM((ROUNDS, NB * S, 2 * S), BF16),
            pltpu.VMEM((NB * S, PL, S), BF16),
        ],
        in_specs=[hbm] * 6,
        out_specs=[vmem] * 3,
        scratch_shapes=[
            pltpu.SMEM((1, NB), jnp.int32),
            pltpu.VMEM((S, 2, S), BF16),
            pltpu.SMEM((1, 2), jnp.int32),
            pltpu.VMEM((S, 2, S), BF16),
            pltpu.SMEM((1, 2), jnp.int32),
            dma((5,)),
            pltpu.VMEM((PL, S, NB, S), BF16),
            pltpu.VMEM((ROWS, NB * S), BF16),
            pltpu.VMEM((2, NB, S, 4 * S), BF16),
            pltpu.VMEM((ROUNDS, 2, 4, 2, S, 2 * S), BF16),
            pltpu.VMEM((256, 256), BF16),
            pltpu.VMEM((AHEAD, NB * S, 2 * S), F32),
            dma((PL,)),
            dma((ROUNDS,)), dma((ROUNDS,)),
            dma(()), dma(()),
            dma(()), dma(()), dma((2, NB)),
            dma(()), dma(()), dma(()), dma((4, 2)),
            dma(()), dma(()),
            dma(()), dma((2, 4)),
            dma((6,)), dma((4, 2)),
            dma(()), dma((2,)),
            dma((ROUNDS,)), dma((ROUNDS, 2)),
        ],
        compiler_params=pltpu.CompilerParams(
            collective_id=0, has_side_effects=True, vmem_limit_bytes=VMEM_LIMIT
        ),
        cost_estimate=pl.CostEstimate(flops=15 << 30, bytes_accessed=8 << 20, transcendentals=0),
    )(
        tensor.reshape(S, PL, NB, S), tensor_mask,
        occ_density.reshape(S, 2, S), occ_mask, virt_density.reshape(S, 2, S), virt_mask,
    )
    out = pl.pallas_call(
        last_kernel,
        out_shape=jax.ShapeDtypeStruct((NB * S, PL, S), BF16),
        in_specs=[vmem] * 3,
        out_specs=pl.BlockSpec(memory_space=pl.ANY),
        scratch_shapes=[pltpu.VMEM((NB * S, PL, S), BF16), dma(())],
        compiler_params=pltpu.CompilerParams(vmem_limit_bytes=LAST_LIMIT),
        cost_estimate=pl.CostEstimate(flops=2 << 30, bytes_accessed=4 << 20, transcendentals=0),
    )(virt, recv, done)
    return out.reshape(NB, S, PL, 1, S)


def solution(mesh):
    placed = (
        P("wide", None, "narrow", None, None),
        P("wide", None),
        P("wide", None, "narrow", None),
        P("wide", "narrow"),
        P("wide", None, "narrow", None),
        P("wide", "narrow"),
    )
    return jax.shard_map(
        shards,
        mesh=mesh,
        in_specs=placed,
        out_specs=P(None, None, "narrow", "wide", None),
        check_vma=False,
    )
```

```python
import functools

import jax
import jax.numpy as jnp
from jax import lax
from jax.experimental import pallas as pl
from jax.experimental.pallas import tpu as pltpu
from jax.sharding import PartitionSpec as P

MESH = pl.DeviceIdType.MESH
BF16 = jnp.bfloat16
F32 = jnp.float32
S = 128
NB = 16
PL = 8
ROUNDS = 4
ROWS = 2 * PL * S
NA = 80
NC = S - NA
VMEM_LIMIT = 47 << 20
LAST_LIMIT = 8 << 20
AHEAD = 2
CHUNK = 4 * S
HALF = NB * S // 2


NEAR = (
    (1, 0), (0, 1), (3, 0), (0, 3), (1, 1), (3, 3), (1, 3), (3, 1),
    (2, 0), (0, 2), (2, 1), (1, 2), (2, 3), (3, 2), (2, 2),
)


def ring(v):
    return lax.rem(v + 4, 4)


def chunk_rows(m):
    return pl.ds(pl.multiple_of(m * CHUNK, CHUNK), CHUNK)


def product(virt, recv, r, m):
    lhs = virt[m].reshape(CHUNK, NB * S)
    return jnp.dot(lhs, recv[r], preferred_element_type=F32).astype(BF16).reshape(CHUNK, 2, S)


def last_kernel(virt, recv, done, out_hbm, outv, out_sem):
    def body(m, c):
        rows = chunk_rows(m)
        outv[rows] = done[rows]
        outv[rows, PL - 2 : PL, :] = product(virt, recv, ROUNDS - 1, m)
        pltpu.make_async_copy(outv.at[rows], out_hbm.at[rows], out_sem).start()
        return c

    lax.fori_loop(0, NB * S // CHUNK, body, 0)
    pltpu.make_async_copy(outv, out_hbm, out_sem).wait()


def kernel(
    t_hbm, tmask_hbm, occ_hbm, omask_hbm, virt_hbm, vmask_hbm, virt, recv, done,
    tmask, occ_ref, omask, virt_ref, vmask, in_sem, traw, tm, occ, send, perm, early,
    t_sem, x_ssem, x_rsem, o1_ssem, o1_rsem, o2_ssem, o3_ssem, o_rsem, c1_ssem, c1_rsem, c2_ssem, c2_rsem,
    v1_ssem, v1_rsem, v1b_ssem, v1b_rsem, v2_ssem, v2_rsem, v3_ssem, v3_rsem,
    a_ssem, a_rsem,
):
    w = lax.axis_index("wide")
    n = lax.axis_index("narrow")
    x, z = w // 4, lax.rem(w, 4)
    y, k = n // 2, lax.rem(n, 2)

    def remote(src, dst, ssem, rsem, wide, narrow):
        return pltpu.make_async_remote_copy(
            src_ref=src, dst_ref=dst, send_sem=ssem, recv_sem=rsem,
            device_id=(wide, narrow), device_id_type=MESH,
        )

    def wait_kib(sem, kib):
        view = recv.at[0, pl.ds(0, kib * 2), :] if kib < 1024 else tm.at[pl.ds(0, kib // 4), :]
        pltpu.make_async_copy(view, view, sem).wait()

    barrier = pltpu.get_barrier_semaphore()
    for dx, dz in reversed(NEAR):
        for e in range(2):
            pl.semaphore_signal(
                barrier,
                inc=1,
                device_id=(ring(x + dx) * 4 + ring(z + dz), y * 2 + e),
                device_id_type=MESH,
            )
    for d in (2, 1, 3):
        pl.semaphore_signal(barrier, inc=1, device_id=(w, ring(y + d) * 2 + k), device_id_type=MESH)
    pl.semaphore_signal(barrier, inc=1, device_id=(w, y * 2 + 1 - k), device_id_type=MESH)

    inputs = [
        pltpu.make_async_copy(src, dst, in_sem.at[t])
        for t, (src, dst) in enumerate(
            (
                (omask_hbm, omask), (occ_hbm, occ_ref), (vmask_hbm, vmask),
                (virt_hbm, virt_ref), (tmask_hbm, tmask),
            )
        )
    ]
    for copy in inputs:
        copy.start()
    for p in range(PL):
        pltpu.make_async_copy(t_hbm.at[:, p], traw.at[p], t_sem.at[p]).start()
    inputs[0].wait()
    inputs[1].wait()

    ycol = pl.ds(pl.multiple_of(y * S, S), S)
    ncol = pl.ds(pl.multiple_of(n * 2 * S, 2 * S), 2 * S)
    wrow = pl.ds(pl.multiple_of(w * S, S), S)
    for j in range(2):
        block = occ_ref[:, j, :].astype(F32) * omask[0, j].astype(F32)
        occ[j, w, :, ycol] = block.astype(BF16)
    pl.semaphore_wait(barrier, 34)

    first, other = pl.ds(0, NA), pl.ds(NA, NC)
    for d in (1, 3, 2):
        for i in range(2):
            own = occ.at[i, w, first, ycol]
            remote(own, own, o1_ssem, o1_rsem, w, ring(y + d) * 2 + k).start()
    for dx, dz in NEAR:
        own = occ.at[:, w, other, ycol]
        remote(own, own, c1_ssem, c1_rsem, ring(x + dx) * 4 + ring(z + dz), n).start()
    place = ((x, z), (z, x))

    def at(i, p, q):
        return p * 4 + q if i == 0 else q * 4 + p

    upper, lower = pl.ds(0, S // 2), pl.ds(S // 2, S // 2)
    def own_rows(r):
        return pl.ds(pl.multiple_of(r * 512 + k * 256, 256), 256)

    def relayout(r):
        for pi in range(2):
            p = 2 * r + pi
            pltpu.make_async_copy(t_hbm.at[:, p], traw.at[p], t_sem.at[p]).wait()

            def body(g, c, p=p, pi=pi):
                pair = jnp.concatenate(
                    [
                        traw[p, pl.ds(pl.multiple_of(g * 32 + h * 16, 16), 16)].reshape(256, S)
                        for h in range(2)
                    ],
                    axis=1,
                )
                got = jnp.dot(perm[...], pair, preferred_element_type=F32).astype(BF16)
                for h in range(2):
                    top = r * 512 + k * 256 + pi * S + g * 32 + h * 16
                    for b in range(NB):
                        tm[pl.ds(pl.multiple_of(top, 16), 16), b * S : (b + 1) * S] = got[
                            b * 16 : (b + 1) * 16, h * S : (h + 1) * S
                        ]
                return c

            lax.fori_loop(0, 4, body, 0)
        mine = tm.at[own_rows(r), :]
        remote(mine, mine, x_ssem.at[r], x_rsem.at[r], w, y * 2 + 1 - k).start()

    def pass_block(i, b, p, q, ssem=o3_ssem):
        part = occ.at[i, b, first, :]
        remote(part, part, ssem, o_rsem.at[i, b], at(i, p, q), n).start()

    def wait_block(i, b):
        part = occ.at[i, b, first, :]
        pltpu.make_async_copy(part, part, o_rsem.at[i, b]).wait()

    def spread(i, yy, d):
        part = occ.at[i, :, other, pl.ds(pl.multiple_of(yy * S, S), S)]
        remote(part, part, c2_ssem, c2_rsem.at[yy, i], w, ring(y + d) * 2 + k).start()

    def wait_spread(i, yy):
        part = occ.at[i, :, other, pl.ds(pl.multiple_of(yy * S, S), S)]
        pltpu.make_async_copy(part, part, c2_rsem.at[yy, i]).wait()

    up, down, far = ring(y + 1), ring(y + 3), ring(y + 2)

    wait_kib(o1_rsem, 6 * NA // 4)
    for d in (1, 3, 2):
        for i in range(2):
            p, q = place[i]
            pass_block(i, w, ring(p + d), q, o2_ssem)
    for i in range(2):
        p, q = place[i]
        for d in (1, 3):
            pass_block(i, w, p, ring(q + d))

    wait_kib(c1_rsem, 15 * NC // 2)
    for i, d in ((0, 3), (1, 1), (0, 1), (1, 3)):
        spread(i, y, d)
    inputs[2].wait()
    inputs[3].wait()
    for j in range(2):
        block = virt_ref[:, j, :].astype(F32) * vmask[0, j].astype(F32)
        virt[x, z, :, pl.ds(pl.multiple_of(n * 2 * S + j * S, S), S)] = block.astype(BF16)
    for d in (1, 3, 2):
        for i, part in enumerate((upper, lower)):
            p, q = place[i]
            own = virt.at[x, z, part, ncol]
            remote(own, own, v1_ssem, v1_rsem, at(i, ring(p + d), q), n).start()

    inputs[4].wait()
    row = lax.broadcasted_iota(jnp.int32, (256, 256), 0)
    col = lax.broadcasted_iota(jnp.int32, (256, 256), 1)
    scale = jnp.zeros((256, 256), F32)
    for b in range(NB):
        scale = scale + jnp.where((row >> 4) == b, 1.0, 0.0) * tmask[0, b].astype(F32)
    hit = jnp.logical_and((row >> 4) == (col & 15), (row & 15) == (col >> 4))
    perm[...] = jnp.where(hit, scale, 0.0).astype(BF16)

    relayout(0)
    for d in (1, 3, 2):
        for i in range(2):
            p, q = place[i]
            b = at(i, ring(p + d), q)
            wait_block(i, b)
            for f in (1, 3):
                pass_block(i, b, p, ring(q + f))
    def line(i, q, h=None):
        part = pl.ds(0, 4) if h is None else pl.ds(2 * h, 2)
        return virt.at[part, q, upper, ncol] if i == 0 else virt.at[q, part, lower, ncol]

    def pass_line(i, q, d, t, h=None):
        ref = line(i, q, h)
        p, here = place[i]
        remote(ref, ref, v1b_ssem, v1b_rsem.at[i, t], at(i, p, ring(here + d)), n).start()

    def wait_line(i, q, t, h=None):
        ref = line(i, q, h)
        pltpu.make_async_copy(ref, ref, v1b_rsem.at[i, t]).wait()

    wait_kib(v1_rsem, 192)
    for i in range(2):
        q = place[i][1]
        pass_line(i, q, 3, 0)
        pass_line(i, q, 1, 1)

    relayout(1)
    wait_spread(0, up)
    spread(0, up, 3)
    wait_spread(1, down)
    spread(1, down, 1)
    for f, g in ((0, 3), (1, 2)):
        for i in range(2):
            p, q = place[i]
            for dq, dp, to in ((1, f, 3), (3, g, 1)):
                b = at(i, ring(p + dp), ring(q + dq))
                wait_block(i, b)
                pass_block(i, b, p, ring(q + to))

    halves = [pl.ds(0, 2), pl.ds(2, 2)]

    def columns(yy, kk):
        return pl.ds(pl.multiple_of((yy * 2 + kk) * 2 * S, 2 * S), 2 * S)

    def to_core(yy, h, t=0):
        part = virt.at[halves[h], :, :, columns(yy, k)]
        remote(part, part, v3_ssem, v3_rsem.at[t], w, y * 2 + 1 - k).start()

    def along(yy, h, d, s):
        part = virt.at[halves[h], :, :, columns(yy, k)]
        remote(part, part, v2_ssem.at[s], v2_rsem.at[lax.rem(yy, 4), h], w, ring(y + d) * 2 + k).start()

    def wait_along(yy, h):
        part = virt.at[halves[h], :, :, columns(yy, k)]
        pltpu.make_async_copy(part, part, v2_rsem.at[yy, h]).wait()

    for i in range(2):
        q = place[i][1]
        wait_line(i, ring(q + 1), 0)
        pass_line(i, ring(q + 1), 3, 2, 0)
        wait_line(i, ring(q + 3), 1)
        pass_line(i, ring(q + 3), 1, 3, 1)
    for i in range(2):
        p, q = place[i]
        for dq, dp in ((1, 3), (1, 2), (3, 0), (3, 1), (2, 0), (2, 1), (2, 2), (2, 3)):
            wait_block(i, at(i, ring(p + dp), ring(q + dq)))
        for yy in (far, up if i == 1 else down):
            wait_spread(i, yy)

    def first_product(r, c):
        theirs = tm.at[pl.ds(pl.multiple_of(r * 512 + (1 - k) * 256, 256), 256), :]
        pltpu.make_async_copy(theirs, theirs, x_rsem.at[r]).wait()
        for j in range(2):
            i = lax.rem(j + x // 2, 2)
            for e in range(2):
                rows = pl.ds(pl.multiple_of(r * 512 + e * 256, 256), 256)
                got = jnp.dot(
                    tm[rows, :], occ[i].reshape(NB * S, 4 * S), preferred_element_type=F32
                ).astype(BF16)
                for xx in range(4):
                    for pi in range(2):
                        send[r, i, xx, e, :, pi * S : (pi + 1) * S] = got[
                            pi * S : (pi + 1) * S, xx * S : (xx + 1) * S
                        ]
                for d in (1, 3, 2, 0):
                    xx = ring(x + d)
                    wide = xx * 4 + 2 * k + i
                    here = jnp.logical_and(wide == w, k == e)
                    src = send.at[r, i, xx, e]
                    dst = recv.at[r, wrow, :]
                    rsem = a_rsem.at[r, x // 2]

                    def away(src=src, dst=dst, rsem=rsem, wide=wide, e=e):
                        remote(src, dst, a_ssem.at[r], rsem, wide, y * 2 + e).start()

                    if d == 0:
                        pl.when(jnp.logical_not(here))(away)

                        @pl.when(here)
                        def _(src=src, dst=dst, rsem=rsem):
                            pltpu.make_async_copy(src, dst, rsem).start()
                    else:
                        away()
        return c

    first_product(0, 0)
    for i in range(2):
        q = place[i][1]
        for h in range(2):
            wait_line(i, ring(q + 2), 2 + h, h)
    along(y, 0, 3, 0)
    along(y, 1, 1, 1)
    along(y, 1, 3, 2)
    along(y, 0, 1, 3)
    to_core(y, 0)
    to_core(y, 1)

    relayout(2)
    relayout(3)
    lax.fori_loop(1, ROUNDS, first_product, 0)

    wait_along(up, 0)
    along(up, 0, 3, 4)
    to_core(up, 0)
    wait_along(down, 1)
    along(down, 1, 1, 5)
    to_core(down, 1)
    wait_along(up, 1)
    to_core(up, 1)
    wait_along(down, 0)
    to_core(down, 0)
    def arrive(r, h):
        half = recv.at[r, pl.ds(pl.multiple_of(h * HALF, HALF), HALF), :]
        pltpu.make_async_copy(half, half, a_rsem.at[r, h]).wait()

    def some(r, m, planes):
        cols = [pl.ds(pl.multiple_of(yy * 4 * S, 4 * S), 4 * S) for yy in planes]
        lhs = jnp.concatenate([virt[m, :, :, c].reshape(CHUNK, 4 * S) for c in cols], axis=1)
        rhs = jnp.concatenate([recv[r, c, :] for c in cols], axis=0)
        return jnp.dot(lhs, rhs, preferred_element_type=F32)

    wait_kib(v3_rsem.at[0], 3072)
    for r in range(AHEAD):
        arrive(r, 0)
        arrive(r, 1)

        def begin(m, c, r=r):
            early[r, chunk_rows(m), :] = some(r, m, (y, up, down))
            return c

        lax.fori_loop(0, NB * S // CHUNK, begin, 0)

    for h in range(2):
        wait_along(far, h)
        to_core(far, h, 1)
    wait_kib(v3_rsem.at[1], 1024)

    for r in range(ROUNDS - 1):
        if r >= AHEAD:
            arrive(r, 0)
            arrive(r, 1)

        def second_product(m, c, r=r):
            rows = chunk_rows(m)
            if r < AHEAD:
                got = (early[r, rows, :] + some(r, m, (far,))).astype(BF16).reshape(CHUNK, 2, S)
            else:
                got = product(virt, recv, r, m)
            done[rows, 2 * r : 2 * r + 2, :] = got
            return c

        lax.fori_loop(0, NB * S // CHUNK, second_product, 0)

    def wait_sent(r):
        local = z // 2 == k

        @pl.when(local)
        def _():
            wait_kib(a_ssem.at[r], 960)

        @pl.when(jnp.logical_not(local))
        def _():
            wait_kib(a_ssem.at[r], 1024)

    wait_kib(o1_ssem, 6 * NA // 4)
    wait_kib(o2_ssem, 6 * NA)
    wait_kib(o3_ssem, 24 * NA)
    wait_kib(c1_ssem, 15 * NC // 2)
    wait_kib(c2_ssem, 24 * NC)
    wait_kib(v1_ssem, 192)
    wait_kib(v1b_ssem, 768)
    for t in range(6):
        wait_kib(v2_ssem.at[t], 512)
    wait_kib(v3_ssem, 4096)
    for r in range(ROUNDS):
        mine = tm.at[own_rows(r), :]
        pltpu.make_async_copy(mine, mine, x_ssem.at[r]).wait()
        if r < ROUNDS - 1:
            wait_sent(r)

    arrive(ROUNDS - 1, 0)
    arrive(ROUNDS - 1, 1)
    wait_sent(ROUNDS - 1)


def shards(tensor, tensor_mask, occ_density, occ_mask, virt_density, virt_mask):
    dma = pltpu.SemaphoreType.DMA
    vmem, hbm = pl.BlockSpec(memory_space=pltpu.VMEM), pl.BlockSpec(memory_space=pl.ANY)
    virt, recv, done = pl.pallas_call(
        kernel,
        out_shape=[
            pltpu.VMEM((4, 4, S, NB * S), BF16),
            pltpu.VMEM((ROUNDS, NB * S, 2 * S), BF16),
            pltpu.VMEM((NB * S, PL, S), BF16),
        ],
        in_specs=[hbm] * 6,
        out_specs=[vmem] * 3,
        scratch_shapes=[
            pltpu.SMEM((1, NB), jnp.int32),
            pltpu.VMEM((S, 2, S), BF16),
            pltpu.SMEM((1, 2), jnp.int32),
            pltpu.VMEM((S, 2, S), BF16),
            pltpu.SMEM((1, 2), jnp.int32),
            dma((5,)),
            pltpu.VMEM((PL, S, NB, S), BF16),
            pltpu.VMEM((ROWS, NB * S), BF16),
            pltpu.VMEM((2, NB, S, 4 * S), BF16),
            pltpu.VMEM((ROUNDS, 2, 4, 2, S, 2 * S), BF16),
            pltpu.VMEM((256, 256), BF16),
            pltpu.VMEM((AHEAD, NB * S, 2 * S), F32),
            dma((PL,)),
            dma((ROUNDS,)), dma((ROUNDS,)),
            dma(()), dma(()),
            dma(()), dma(()), dma((2, NB)),
            dma(()), dma(()), dma(()), dma((4, 2)),
            dma(()), dma(()),
            dma(()), dma((2, 4)),
            dma((6,)), dma((4, 2)),
            dma(()), dma((2,)),
            dma((ROUNDS,)), dma((ROUNDS, 2)),
        ],
        compiler_params=pltpu.CompilerParams(
            collective_id=0, has_side_effects=True, vmem_limit_bytes=VMEM_LIMIT
        ),
        cost_estimate=pl.CostEstimate(flops=15 << 30, bytes_accessed=8 << 20, transcendentals=0),
    )(
        tensor.reshape(S, PL, NB, S), tensor_mask,
        occ_density.reshape(S, 2, S), occ_mask, virt_density.reshape(S, 2, S), virt_mask,
    )
    out = pl.pallas_call(
        last_kernel,
        out_shape=jax.ShapeDtypeStruct((NB * S, PL, S), BF16),
        in_specs=[vmem] * 3,
        out_specs=pl.BlockSpec(memory_space=pl.ANY),
        scratch_shapes=[pltpu.VMEM((NB * S, PL, S), BF16), dma(())],
        compiler_params=pltpu.CompilerParams(vmem_limit_bytes=LAST_LIMIT),
        cost_estimate=pl.CostEstimate(flops=2 << 30, bytes_accessed=4 << 20, transcendentals=0),
    )(virt, recv, done)
    return out.reshape(NB, S, PL, 1, S)


def solution(mesh):
    placed = (
        P("wide", None, "narrow", None, None),
        P("wide", None),
        P("wide", None, "narrow", None),
        P("wide", "narrow"),
        P("wide", None, "narrow", None),
        P("wide", "narrow"),
    )
    return jax.shard_map(
        shards,
        mesh=mesh,
        in_specs=placed,
        out_specs=P(None, None, "narrow", "wide", None),
        check_vma=False,
    )
```
